256 devices in a mesh: group: 8 (over z), dev: 32 (over x, y, core).
Axes of the slice: x: 4, y: 4, z: 8, core: 2. Of those that a mesh axis runs over, the one named last changes fastest.
Arguments:
- corpus_rows: bfloat16 [524288, 1024], P(('group', 'dev')), may hold values from -16 to 16
- list_ids: int32 [524288], P(('group', 'dev')), may hold values from 0 to 65535, as said below
- source_ids: int32 [524288], P(('group', 'dev')), may hold values from 0 to 999999
- list_slot: int32 [65536], replicated, may hold values from 0 to 65535, as said below
- centroids: bfloat16 [65536, 1024], P('dev'), may hold values from -13 to 13
- start_basis: float32 [1024, 256], replicated, may hold values from -6 to 6
Outputs:
- row_codes: bfloat16 [1310720, 256], P(('group', 'dev'))
- row_sources: int32 [1310720], P(('group', 'dev'))
- list_counts: int32 [65536], P('dev')
The draws below stay inside these ranges and needn't reach their ends.
Inputs may be any that keep to these rules, and one draw needn't show every extreme that they name: A permutation; the centroid of list l is row list_slot[l] of centroids. For each device, at most 160 of its rows have an owner list_slot[list_ids] // 2048 equal to any one index o; in every draw one owner of each group takes exactly 160 rows from every device of that group.
All inputs are finite; a program needn't handle non-finite values.
Results may differ from the reference program's by a relative error of at most 0.001.
Values may be sent and summed in bfloat16 or wider, within the bound.
A program may use at most 128 MiB of HBM per device.

```python
import jax
import jax.numpy as jnp
from jax import lax

D = 1024
RANK = 256
LISTS_DEV = 2048
ITERS = 2
ROWS_DEV = 2048
SENDERS = 256
ROWS = 524288
LISTS = 65536
CAP = 160
N_GROUP = 8
N_DEV = 32


def shared_slots(key):
    return jax.random.permutation(jax.random.fold_in(key, 11), LISTS).astype(jnp.int32)


def column_scales(key):
    return jnp.exp(jax.random.uniform(jax.random.fold_in(key, 13), (D,), jnp.float32, -0.5, 0.5))


def centroid_table(key):
    values = jnp.clip(jax.random.normal(jax.random.fold_in(key, 17), (LISTS, D), jnp.float32), -2.5, 2.5)
    return 3.0 * values * column_scales(key)[None, :]


def draw_list_slot(key, part):
    return shared_slots(key)


def draw_centroids(key, part):
    return centroid_table(key).astype(jnp.bfloat16)


def draw_list_ids(key, part):
    slot_of_list = shared_slots(key)
    key = jax.random.fold_in(key, 5)
    subkeys = jax.random.split(key, 5)
    owner_total = LISTS // LISTS_DEV
    groups = SENDERS // owner_total
    list_of_slot = jnp.zeros((LISTS,), jnp.int32).at[slot_of_list].set(jnp.arange(LISTS, dtype=jnp.int32))
    hot_owner = jax.random.randint(subkeys[0], (groups,), 0, owner_total).astype(jnp.int32)
    shuffled = jax.vmap(lambda subkey: jax.random.permutation(subkey, ROWS_DEV))(jax.random.split(subkeys[1], SENDERS)).astype(jnp.int32)
    jitter = jax.random.randint(subkeys[2], (SENDERS, ROWS_DEV), 0, 2).astype(jnp.int32)
    remaining = shuffled - CAP
    spread = (remaining + jitter) % (owner_total - 1)
    group_hot = jnp.take(hot_owner, jnp.arange(SENDERS, dtype=jnp.int32) // owner_total)[:, None]
    others_id = spread + (spread >= group_hot).astype(jnp.int32)
    owner_of = jnp.where(shuffled < CAP, group_hot, others_id)
    first_pick = jax.random.randint(subkeys[3], (SENDERS, ROWS_DEV), 0, LISTS_DEV).astype(jnp.int32)
    second_pick = jax.random.randint(subkeys[4], (SENDERS, ROWS_DEV), 0, LISTS_DEV).astype(jnp.int32)
    slot_ids = owner_of * LISTS_DEV + jnp.minimum(first_pick, second_pick)
    return jnp.take(list_of_slot, slot_ids.reshape(ROWS))


def draw_corpus_rows(key, part):
    list_rows = draw_list_ids(key, part)
    slot_rows = jnp.take(shared_slots(key), list_rows)
    centres = jnp.take(centroid_table(key).astype(jnp.bfloat16).astype(jnp.float32), slot_rows, axis=0)
    scale_row = column_scales(key)[None, :]
    key = jax.random.fold_in(key, 7)
    values = jnp.clip(jax.random.normal(key, (ROWS, D), jnp.float32), -5.0, 5.0)
    return (centres + 0.25 * values * scale_row).astype(jnp.bfloat16)


def plant(result, key, least, top_value):
    place = [jax.random.randint(jax.random.fold_in(key, axis), (), 0, length) for axis, length in enumerate(result.shape)]
    main_axis = result.shape.index(max(result.shape))
    beside = place[:main_axis] + [(place[main_axis] + 1) % result.shape[main_axis]] + place[main_axis + 1:]
    return result.at[tuple(place)].set(least).at[tuple(beside)].set(top_value)


def centred(rng, shape, width, most, kind=jnp.bfloat16):
    entries = jax.random.normal(rng, shape, jnp.float32) * width
    return jnp.minimum(jnp.maximum(entries, -most), most).astype(kind)


def setup_inputs(seed: int = 0) -> dict:
    splits = jax.random.split(jax.random.key(seed), 7)
    return {
        "corpus_rows": draw_corpus_rows(jax.random.fold_in(splits[6], 71), 0),
        "list_ids": draw_list_ids(jax.random.fold_in(splits[6], 71), 0),
        "source_ids": plant(jax.random.randint(splits[2], (ROWS,), 0, 1000000), jax.random.fold_in(splits[2], 1), 0, 999999).astype(jnp.int32),
        "list_slot": draw_list_slot(jax.random.fold_in(splits[6], 71), 0),
        "centroids": draw_centroids(jax.random.fold_in(splits[6], 71), 0),
        "start_basis": centred(splits[5], (D, RANK), 1.0, 6.0, jnp.float32),
    }


exact_mode = lax.Precision.HIGHEST

def orthonormal(product):
    gram_matrix = jnp.dot(product.T.astype(jnp.float32), product.astype(jnp.float32), precision=exact_mode, preferred_element_type=jnp.float32)
    factor = jnp.linalg.cholesky(gram_matrix)
    return jax.scipy.linalg.solve_triangular(factor, product.T, lower=True).T

def reference(corpus_rows, list_ids, source_ids, list_slot, centroids, start_basis):
    senders = N_GROUP * N_DEV
    blocks = corpus_rows.reshape(senders, ROWS_DEV, D)

    def accumulate(running, row_block):
        term = lax.dot_general(row_block.astype(jnp.float32), row_block.astype(jnp.float32), (((0,), (0,)), ((), ())), preferred_element_type=jnp.float32)
        return (running + term, None)
    moment, _ = lax.scan(accumulate, jnp.zeros((D, D), jnp.float32), blocks)
    basis_now = start_basis
    for sweep in range(ITERS):
        product = jnp.dot(moment.astype(jnp.float32), basis_now.astype(jnp.float32), precision=exact_mode, preferred_element_type=jnp.float32)
        basis_now = orthonormal(product)
    slot_ids = jnp.take(list_slot, list_ids).astype(jnp.int32)
    owner_of = (slot_ids // LISTS_DEV).reshape(senders, ROWS_DEV)
    onehot = (owner_of[:, :, None] == jnp.arange(N_DEV, dtype=jnp.int32)[None, None, :]).astype(jnp.int32)
    order_rank = jnp.sum(onehot * (jnp.cumsum(onehot, axis=1) - 1), axis=2)
    sender = jnp.arange(senders, dtype=jnp.int32)[:, None]
    group_of = sender // N_DEV
    within = sender % N_DEV
    target = (((group_of * N_DEV + owner_of) * N_DEV + within) * CAP + order_rank).reshape(-1)

    def encode(pair):
        row_block, block_slots = pair
        residual_rows = row_block.astype(jnp.float32) - jnp.take(centroids, block_slots, axis=0).astype(jnp.float32)
        return jnp.dot(residual_rows.astype(jnp.float32), basis_now.astype(jnp.float32), precision=exact_mode, preferred_element_type=jnp.float32).astype(jnp.bfloat16)
    encoded = lax.map(encode, (blocks, slot_ids.reshape(senders, ROWS_DEV)))
    total_slots = senders * N_DEV * CAP
    row_codes = jnp.zeros((total_slots, RANK), jnp.bfloat16).at[target].set(encoded.reshape(-1, RANK))
    row_sources = jnp.full((total_slots,), -1, jnp.int32).at[target].set(source_ids)
    list_counts = jnp.zeros((LISTS_DEV * N_DEV,), jnp.int32).at[slot_ids].add(1)
    return (row_codes, row_sources, list_counts)
```

```python
import functools
import jax, jax.numpy as jnp
from jax import lax
from jax.experimental import pallas as pl
from jax.experimental.pallas import tpu as pltpu
MESH = pl.DeviceIdType.MESH
from jax.sharding import PartitionSpec as P
NX, NY, NZ = 4, 4, 8
HALF, PART, MID, LOW = 2304, 1152, 288, 72


def reduce_kernel(part_ref, out_ref, core_buf, big_buf, mid_buf, tile_buf, core_s, core_r, big_s, big_r, mid_s, mid_r,
                  tile_s, tile_r, up_s, up_r):
    z = lax.axis_index("group")
    dev = lax.axis_index("dev")
    x, y, c = dev // 8, (dev // 2) % 4, dev % 2

    def at(xx, yy, cc, zz):
        return (zz, (xx * 4 + yy) * 2 + cc)

    other = at(x, y, 1 - c, z)
    along_x = [at((x + d) % 4, y, c, z) for d in (1, 2, 3)]
    along_y = [at(x, (y + d) % 4, c, z) for d in (1, 2, 3)]
    along_z = [at(x, y, c, (z + d) % 8) for d in range(1, 8)]
    barrier = pltpu.get_barrier_semaphore()
    for peer in [other] + along_x + along_y + along_z:
        pl.semaphore_signal(barrier, inc=1, device_id=peer, device_id_type=MESH)
    pl.semaphore_wait(barrier, 14)

    def send(src, dst, s, r, peer):
        copy = pltpu.make_async_remote_copy(src_ref=src, dst_ref=dst, send_sem=s, recv_sem=r, device_id=peer,
                                            device_id_type=MESH)
        copy.start()
        return copy

    def rows(ref, start, size):
        return ref.at[pl.ds(pl.multiple_of(start, 8), size)]

    mine, theirs = c * HALF, (1 - c) * HALF
    first = [(x, along_x), (y, along_y)]
    second = [(y, along_y), (x, along_x)]
    core = [send(rows(part_ref, theirs + p * PART, PART), core_buf.at[p], core_s.at[p], core_r.at[p], other)
            for p in range(2)]
    big = [[], []]
    for p in range(2):
        core[p].wait_recv()
        core_buf[p] = core_buf[p] + part_ref[pl.ds(pl.multiple_of(mine + p * PART, 8), PART)]
        pos, peers = first[p]
        for d in (1, 2, 3):
            big[p].append(send(rows(core_buf.at[p], ((pos + d) % 4) * MID, MID), big_buf.at[p, d - 1],
                               big_s.at[p, d - 1], big_r.at[p, d - 1], peers[d - 1]))
    mid = [[], []]
    for p in range(2):
        for copy in big[p]:
            copy.wait_recv()
        pos, peers = first[p]
        own = core_buf[p, pl.ds(pl.multiple_of(pos * MID, 8), MID)]
        big_buf[p, 3] = (own + big_buf[p, 0]) + (big_buf[p, 1] + big_buf[p, 2])
        pos, peers = second[p]
        for d in (1, 2, 3):
            mid[p].append(send(rows(big_buf.at[p, 3], ((pos + d) % 4) * LOW, LOW), mid_buf.at[p, d - 1],
                               mid_s.at[p, d - 1], mid_r.at[p, d - 1], peers[d - 1]))
    tile = [[], []]
    for p in range(2):
        for copy in mid[p]:
            copy.wait_recv()
        pos, peers = second[p]
        own = big_buf[p, 3, pl.ds(pl.multiple_of(pos * LOW, 8), LOW)]
        mid_buf[p, 3] = (own + mid_buf[p, 0]) + (mid_buf[p, 1] + mid_buf[p, 2])
        for d in range(1, 8):
            tile[p].append(send(rows(mid_buf.at[p, 3], ((z + d) % 8) * 8, 8), tile_buf.at[p, d - 1, 0],
                                tile_s.at[p, d - 1, 0], tile_r.at[p, d - 1, 0], along_z[d - 1]))
            tile[p].append(send(mid_buf.at[p, 3, pl.ds(64, 8)], tile_buf.at[p, d - 1, 1],
                                tile_s.at[p, d - 1, 1], tile_r.at[p, d - 1, 1], along_z[d - 1]))
    up = [[], []]

    def spread(p, start, size, peers, base):
        for i, peer in enumerate(peers):
            up[p].append(send(rows(out_ref, start, size), rows(out_ref, start, size), up_s.at[p, base + i],
                              up_r.at[p, base + i], peer))

    start = []
    for p in range(2):
        for copy in tile[p]:
            copy.wait_recv()
        begin = mine + p * PART + first[p][0] * MID + second[p][0] * LOW
        start.append(begin)
        own = mid_buf[p, 3, pl.ds(pl.multiple_of(z * 8, 8), 8)]
        last = mid_buf[p, 3, pl.ds(64, 8)]
        for d in range(7):
            own = own + tile_buf[p, d, 0]
        out_ref[pl.ds(pl.multiple_of(begin + z * 8, 8), 8)] = own
        seq = [last] + [tile_buf[p, d, 1] for d in range(7)]
        tot = jnp.zeros((8, 128), jnp.float32)
        for k in range(8):
            term = seq[0]
            for d in range(1, 8):
                term = jnp.where((z - k + 8) % 8 == d, seq[d], term)
            tot = tot + term
        out_ref[pl.ds(pl.multiple_of(begin + 64, 8), 8)] = tot
        spread(p, begin + z * 8, 8, along_z, 0)
    for p in range(2):
        for copy in up[p][0:7]:
            copy.wait_recv()
        spread(p, start[p], LOW, second[p][1], 7)
    for p in range(2):
        for copy in up[p][7:10]:
            copy.wait_recv()
        spread(p, mine + p * PART + first[p][0] * MID, MID, first[p][1], 10)
    for p in range(2):
        for copy in up[p][10:13]:
            copy.wait_recv()
        spread(p, mine + p * PART, PART, [other], 13)
    for p in range(2):
        up[p][13].wait_recv()
    for p in range(2):
        for copy in [core[p]] + big[p] + mid[p] + tile[p] + up[p]:
            copy.wait_send()


def reduce_moment(part):
    sem = pltpu.SemaphoreType.DMA
    return pl.pallas_call(
        reduce_kernel,
        out_shape=jax.ShapeDtypeStruct(part.shape, jnp.float32),
        in_specs=[pl.BlockSpec(memory_space=pltpu.VMEM)],
        out_specs=pl.BlockSpec(memory_space=pltpu.VMEM),
        scratch_shapes=[
            pltpu.VMEM((2, PART, 128), jnp.float32),
            pltpu.VMEM((2, 4, MID, 128), jnp.float32),
            pltpu.VMEM((2, 4, LOW, 128), jnp.float32),
            pltpu.VMEM((2, 7, 2, 8, 128), jnp.float32),
            sem((2,)), sem((2,)), sem((2, 3)), sem((2, 3)), sem((2, 3)), sem((2, 3)),
            sem((2, 7, 2)), sem((2, 7, 2)), sem((2, 14)), sem((2, 14)),
        ],
        compiler_params=pltpu.CompilerParams(collective_id=0, has_side_effects=True, vmem_limit_bytes=32 * 2**20),
        cost_estimate=pl.CostEstimate(flops=10**6, bytes_accessed=10**8, transcendentals=0),
        name="reduce_moment",
    )(part)


CAP_OF = 160


def dot(a, b, dims=(((1,), (0,)), ((), ()))):
    return lax.dot_general(a, b, dims, preferred_element_type=jnp.float32)


def halves(v):
    top = v.astype(jnp.bfloat16)
    return top, (v - top.astype(jnp.float32)).astype(jnp.bfloat16)


def vmem():
    return pl.BlockSpec(memory_space=pltpu.VMEM)


def smem():
    return pl.BlockSpec(memory_space=pltpu.SMEM)


def limits():
    return pltpu.CompilerParams(vmem_limit_bytes=48 * 2**20)


NT = (((1,), (1,)), ((), ()))
TN = (((0,), (0,)), ((), ()))


def place_kernel(lists_dev, cap, list_ref, source_ref, table_ref, pos_ref, dest_ref):
    count = list_ref.shape[1]
    owners = dest_ref.shape[0]
    table_rows = table_ref.shape[0]
    ids = list_ref[...]
    sub = lax.broadcasted_iota(jnp.int32, (table_rows, count), 0)
    row_hit = (sub == ids // 128).astype(jnp.bfloat16)
    table = table_ref[...]
    high = dot((table // 256).astype(jnp.float32).astype(jnp.bfloat16), row_hit, TN)
    low = dot((table % 256).astype(jnp.float32).astype(jnp.bfloat16), row_hit, TN)
    lane = lax.broadcasted_iota(jnp.int32, (128, count), 0)
    slot = jnp.sum(jnp.where(lane == ids % 128, high * 256.0 + low, 0.0), axis=0, keepdims=True).astype(jnp.int32)
    owner = slot // lists_dev
    local = slot % lists_dev
    owner_hit = lax.broadcasted_iota(jnp.int32, (owners, count), 0) == owner
    owner_one = owner_hit.astype(jnp.float32).astype(jnp.bfloat16)
    width = 256
    before = (
        lax.broadcasted_iota(jnp.int32, (width, width), 0) < lax.broadcasted_iota(jnp.int32, (width, width), 1)
    ).astype(jnp.float32).astype(jnp.bfloat16)
    seen = jnp.zeros((owners, 1), jnp.float32)
    ranks = []
    for k in range(count // width):
        part = owner_one[:, k * width:(k + 1) * width]
        prior = dot(part, before) + seen
        part = part.astype(jnp.float32)
        ranks.append(jnp.sum(prior * part, axis=0, keepdims=True))
        seen = seen + jnp.sum(part, axis=1, keepdims=True)
    rank = jnp.concatenate(ranks, axis=1).astype(jnp.int32)
    pos_ref[...] = owner * cap + rank
    rank_hit = lax.broadcasted_iota(jnp.int32, (cap, count), 0) == rank
    source = source_ref[...]

    def collect(value):
        picked = jnp.where(rank_hit, value.astype(jnp.float32), 0.0).astype(jnp.bfloat16)
        return dot(owner_one, picked, NT)

    filled = collect(jnp.ones((1, count), jnp.int32)) > 0.5
    local_at = collect(local // 256) * 256.0 + collect(local % 256)
    source_at = collect(source // 16384) * 16384.0 + collect((source // 128) % 128) * 128.0 + collect(source % 128)
    dest_ref[:, 0:cap] = jnp.where(filled, local_at, -1.0).astype(jnp.int32)
    dest_ref[:, 256:256 + cap] = jnp.where(filled, source_at, -1.0).astype(jnp.int32)


def place(list_ids, source_ids, list_slot, owners, lists_dev, cap):
    count = list_ids.shape[0]
    return pl.pallas_call(
        functools.partial(place_kernel, lists_dev, cap),
        out_shape=(jax.ShapeDtypeStruct((1, count), jnp.int32), jax.ShapeDtypeStruct((owners, 512), jnp.int32)),
        in_specs=[vmem(), vmem(), vmem()],
        out_specs=(vmem(), vmem()),
        compiler_params=limits(),
        name="place",
    )(list_ids.reshape(1, count), source_ids.reshape(1, count), list_slot.reshape(-1, 128))


def moment_kernel(x_ref, out_ref):
    step = pl.program_id(0)

    @pl.when(step == 0)
    def _():
        out_ref[...] = jnp.zeros_like(out_ref)

    for i in range(4):
        left = x_ref[:, i * 256:(i + 1) * 256].T
        for j in range(i + 1):
            square = dot(left, x_ref[:, j * 256:(j + 1) * 256])
            for a in range(2):
                for b in range(2):
                    row, col = 2 * i + a, 2 * j + b
                    if col <= row:
                        at = (row * (row + 1) // 2 + col) * 128
                        out_ref[at:at + 128, :] += square[a * 128:(a + 1) * 128, b * 128:(b + 1) * 128]


def local_moment(x):
    steps = 4
    return pl.pallas_call(
        moment_kernel,
        out_shape=jax.ShapeDtypeStruct((4608, 128), jnp.float32),
        grid=(steps,),
        in_specs=[pl.BlockSpec((x.shape[0] // steps, x.shape[1]), lambda s: (s, 0))],
        out_specs=pl.BlockSpec((4608, 128), lambda s: (0, 0)),
        compiler_params=limits(),
        name="local_moment",
    )(x)


def project_kernel(tri_ref, start_ref, x_ref, pos_ref, out_ref, basis_ref, gram_ref, m_hi, m_lo, z_ref):
    eye = lax.broadcasted_iota(jnp.int32, (128, 128), 0) == lax.broadcasted_iota(jnp.int32, (128, 128), 1)
    peak = jnp.zeros((128, 128), jnp.float32)
    for i in range(8):
        for j in range(i + 1):
            at = (i * (i + 1) // 2 + j) * 128
            block = tri_ref[at:at + 128, :]
            hi, lo = halves(block)
            m_hi[i * 128:(i + 1) * 128, j * 128:(j + 1) * 128] = hi
            m_lo[i * 128:(i + 1) * 128, j * 128:(j + 1) * 128] = lo
            if i != j:
                hi, lo = halves(block.T)
                m_hi[j * 128:(j + 1) * 128, i * 128:(i + 1) * 128] = hi
                m_lo[j * 128:(j + 1) * 128, i * 128:(i + 1) * 128] = lo
            else:
                peak = jnp.maximum(peak, jnp.where(eye, block, 0.0))
    scale = 1.0 / jnp.max(jnp.max(peak, axis=0, keepdims=True), axis=1, keepdims=True)
    width = start_ref.shape[1]

    def times_moment(v):
        hi, lo = halves(v * scale)
        both = dot(m_hi[...], jnp.concatenate([hi, lo], axis=1))
        return (both[:, :width] + both[:, width:]) + dot(m_lo[...], hi)

    product = times_moment(times_moment(start_ref[...]))
    product = product * lax.rsqrt(jnp.sum(product * product, axis=0, keepdims=True))
    hi, lo = halves(product)
    basis_ref[:, :width] = hi
    basis_ref[:, width:] = lo
    cross = dot(hi, basis_ref[...], TN)
    mixed = cross[:, width:]
    gram_ref[...] = cross[:, :width] + (mixed + mixed.T)
    step = 256

    @pl.loop(0, x_ref.shape[0] // step)
    def _(k):
        at = pl.ds(pl.multiple_of(k * step, step), step)
        both = dot(x_ref[at, :], basis_ref[...])
        z_ref[at, :] = both[:, :width] + both[:, width:]

    @pl.loop(0, x_ref.shape[0] // 16)
    def _(k):
        for u in range(16):
            out_ref[pl.ds(pos_ref[0, k * 16 + u], 1), :] = z_ref[pl.ds(k * 16 + u, 1), :]


def project(tri, start, x, pos, slots):
    feature, width = start.shape
    return pl.pallas_call(
        project_kernel,
        out_shape=(
            jax.ShapeDtypeStruct((slots, width), jnp.float32),
            jax.ShapeDtypeStruct((feature, 2 * width), jnp.bfloat16),
            jax.ShapeDtypeStruct((width, width), jnp.float32),
        ),
        in_specs=[vmem(), vmem(), vmem(), smem()],
        out_specs=(vmem(), vmem(), vmem()),
        scratch_shapes=[
            pltpu.VMEM((feature, feature), jnp.bfloat16),
            pltpu.VMEM((feature, feature), jnp.bfloat16),
            pltpu.VMEM((x.shape[0], width), jnp.float32),
        ],
        compiler_params=limits(),
        cost_estimate=pl.CostEstimate(flops=10**10, bytes_accessed=2 * 10**7, transcendentals=0),
        name="project",
    )(tri, start, x, pos)


def factor_kernel(gram_ref, inverse_ref, pivot_ref, aug):
    size = gram_ref.shape[0]
    block = 32
    panel = 8
    aug[:, :size] = gram_ref[...]
    aug[:, size:] = (
        lax.broadcasted_iota(jnp.int32, (size, size), 0) == lax.broadcasted_iota(jnp.int32, (size, size), 1)
    ).astype(jnp.float32)
    row_at = lax.broadcasted_iota(jnp.int32, (block, 128), 0)
    lane_at = lax.broadcasted_iota(jnp.int32, (block, 128), 1)
    least = jnp.full((1, 128), 1e30, jnp.float32)
    for b in range(size // block):
        lo, hi = b * block, (b + 1) * block
        square = aug[lo:hi, lo:hi]
        unit = (row_at[:, :block] == lane_at[:, :block]).astype(jnp.float32)
        work = jnp.concatenate([square, unit, jnp.zeros((block, 128 - 2 * block), jnp.float32)], axis=1)
        for p in range(block // panel):
            cols = [
                jnp.broadcast_to(work[:, p * panel + j:p * panel + j + 1], (block, 128)) for j in range(panel)
            ]
            for j in range(panel):
                k = p * panel + j
                pivot = cols[j][k:k + 1, :]
                least = jnp.minimum(least, pivot)
                root = lax.rsqrt(pivot)
                column = jnp.where(row_at > k, cols[j] * root, 0.0)
                for jj in range(j + 1, panel):
                    kk = p * panel + jj
                    cols[jj] = cols[jj] - column * column[kk:kk + 1, :]
                row = work[k:k + 1, :] * root
                work = jnp.where(row_at == k, row, work - column * row)
        inverse = work[:, block:2 * block]
        rows = lax.dot_general(inverse, aug[lo:hi, :], (((1,), (0,)), ((), ())), precision=lax.Precision.HIGHEST,
                               preferred_element_type=jnp.float32)
        aug[lo:hi, :] = rows
        if hi < size:
            below = rows[:, hi:size].T
            aug[hi:, :] -= lax.dot_general(below, rows, (((1,), (0,)), ((), ())), precision=lax.Precision.HIGHEST,
                                           preferred_element_type=jnp.float32)
    whole = aug[:, size:].T
    top, bottom = halves(whole)
    inverse_ref[:, :size] = top
    inverse_ref[:, size:] = bottom
    pivot_ref[...] = least


def factor(gram):
    size = gram.shape[0]
    return pl.pallas_call(
        factor_kernel,
        out_shape=(
            jax.ShapeDtypeStruct((size, 2 * size), jnp.bfloat16),
            jax.ShapeDtypeStruct((1, 128), jnp.float32),
        ),
        in_specs=[vmem()],
        out_specs=(vmem(), vmem()),
        scratch_shapes=[pltpu.VMEM((size, 2 * size), jnp.float32)],
        compiler_params=limits(),
        cost_estimate=pl.CostEstimate(flops=10**9, bytes_accessed=10**7, transcendentals=0),
        name="factor",
    )(gram)


def offset_kernel(c_ref, basis_ref, id_ref, out_ref, z_ref):
    width = out_ref.shape[1]
    step = 256

    @pl.loop(0, c_ref.shape[0] // step)
    def _(k):
        at = pl.ds(pl.multiple_of(k * step, step), step)
        both = dot(c_ref[at, :], basis_ref[...])
        z_ref[at, :] = both[:, :width] + both[:, width:]

    @pl.loop(0, out_ref.shape[0] // 16)
    def _(k):
        for u in range(16):
            at = jnp.maximum(id_ref[k * 16 + u], 0)
            out_ref[pl.ds(k * 16 + u, 1), :] = z_ref[pl.ds(at, 1), :]


def offsets_at(centroids, basis, ids):
    width = basis.shape[1] // 2
    return pl.pallas_call(
        offset_kernel,
        out_shape=jax.ShapeDtypeStruct((ids.shape[0], width), jnp.float32),
        in_specs=[vmem(), vmem(), smem()],
        out_specs=vmem(),
        scratch_shapes=[pltpu.VMEM((centroids.shape[0], width), jnp.float32)],
        compiler_params=limits(),
        cost_estimate=pl.CostEstimate(flops=10**10, bytes_accessed=10**7, transcendentals=0),
        name="offsets",
    )(centroids, basis, ids)


def finish_kernel(z_ref, off_ref, id_ref, inverse_ref, out_ref):
    width = z_ref.shape[1]
    hi, lo = halves(z_ref[...] - off_ref[...])
    both = dot(hi, inverse_ref[...])
    code = (both[:, :width] + both[:, width:]) + dot(lo, inverse_ref[:, :width])
    out_ref[...] = jnp.where(id_ref[...] >= 0, code, 0.0).astype(jnp.bfloat16)


def finish(z, off, ids, inverse):
    slots, width = z.shape
    step = 512
    return pl.pallas_call(
        finish_kernel,
        out_shape=jax.ShapeDtypeStruct((slots, width), jnp.bfloat16),
        grid=(slots // step,),
        in_specs=[
            pl.BlockSpec((step, width), lambda s: (s, 0)),
            pl.BlockSpec((step, width), lambda s: (s, 0)),
            pl.BlockSpec((step, 1), lambda s: (s, 0)),
            pl.BlockSpec((width, 2 * width), lambda s: (0, 0)),
        ],
        out_specs=pl.BlockSpec((step, width), lambda s: (s, 0)),
        compiler_params=limits(),
        cost_estimate=pl.CostEstimate(flops=2 * 10**9, bytes_accessed=13 * 10**6, transcendentals=0),
        name="finish",
    )(z, off, ids.reshape(slots, 1), inverse)


def tally_kernel(id_ref, out_ref):
    ids = id_ref[...]
    count = ids.shape[1]
    high = lax.broadcasted_iota(jnp.int32, (16, count), 0) == jnp.where(ids >= 0, ids // 128, -1)
    low = lax.broadcasted_iota(jnp.int32, (128, count), 0) == ids % 128
    out_ref[...] = dot(high.astype(jnp.float32).astype(jnp.bfloat16), low.astype(jnp.float32).astype(jnp.bfloat16), NT)


def tally(ids):
    return pl.pallas_call(
        tally_kernel,
        out_shape=jax.ShapeDtypeStruct((16, 128), jnp.float32),
        in_specs=[vmem()],
        out_specs=vmem(),
        compiler_params=limits(),
        cost_estimate=pl.CostEstimate(flops=10**7, bytes_accessed=10**6, transcendentals=0),
        name="tally",
    )(ids.reshape(1, -1))


exact_mode = lax.Precision.HIGHEST
PIVOT_LEAST = 1.0 / 64.0


def orthonormal(product):
    gram_matrix = jnp.dot(product.T, product, precision=exact_mode, preferred_element_type=jnp.float32)
    lower = jnp.linalg.cholesky(gram_matrix)
    return jax.scipy.linalg.solve_triangular(lower, product.T, lower=True).T


def careful(tri, start, x, centroids, pos, ids):
    owners = lax.axis_size("dev")
    slots = ids.shape[0]
    grid = [[None] * 8 for _ in range(8)]
    for i in range(8):
        for j in range(i + 1):
            at = (i * (i + 1) // 2 + j) * 128
            grid[i][j] = tri[at:at + 128]
            grid[j][i] = tri[at:at + 128].T
    moment = jnp.block(grid)
    basis = start
    for sweep in range(2):
        product = jnp.dot(moment, basis, precision=exact_mode, preferred_element_type=jnp.float32)
        basis = orthonormal(product)
    width = start.shape[1]
    projected = jnp.dot(x, basis, precision=exact_mode, preferred_element_type=jnp.float32)
    sent = jnp.zeros((slots, width), jnp.float32).at[pos.reshape(-1)].set(projected)
    sent = sent.reshape(owners, slots // owners, width)
    values = lax.all_to_all(sent, "dev", split_axis=0, concat_axis=0, tiled=True).reshape(slots, width)
    offsets = jnp.dot(centroids, basis, precision=exact_mode, preferred_element_type=jnp.float32)
    code = values - jnp.take(offsets, jnp.maximum(ids, 0), axis=0)
    return jnp.where(ids[:, None] >= 0, code, 0.0).astype(jnp.bfloat16)


def shards(corpus_rows, list_ids, source_ids, list_slot, centroids, start_basis):
    owners = lax.axis_size("dev")
    lists_dev = centroids.shape[0]
    cap = CAP_OF
    slots = owners * cap
    pos, dest = place(list_ids, source_ids, list_slot, owners, lists_dev, cap)
    arrived = lax.all_to_all(dest, "dev", split_axis=0, concat_axis=0, tiled=True)
    tri = reduce_moment(local_moment(corpus_rows))
    sent, basis, gram = project(tri, start_basis, corpus_rows, pos, slots)
    width = start_basis.shape[1]
    values = lax.all_to_all(
        sent.reshape(owners, cap, width), "dev", split_axis=0, concat_axis=0, tiled=True
    ).reshape(slots, width)
    ids = arrived[:, :cap].reshape(slots)
    row_sources = arrived[:, 256:256 + cap].reshape(slots)
    tallies = lax.all_gather(tally(ids), "group")
    inverse, pivots = factor(gram)
    off = offsets_at(centroids, basis, ids)
    row_codes = lax.cond(
        jnp.min(pivots) >= PIVOT_LEAST,
        lambda: finish(values, off, ids, inverse),
        lambda: careful(tri, start_basis, corpus_rows, centroids, pos, ids),
    )
    list_counts = jnp.sum(tallies, axis=0).astype(jnp.int32).reshape(lists_dev)
    return row_codes, row_sources, list_counts


def solution(mesh):
    placed = (
        P(("group", "dev"), None),
        P(("group", "dev")),
        P(("group", "dev")),
        P(),
        P("dev", None),
        P(),
    )
    return jax.shard_map(
        shards,
        mesh=mesh,
        in_specs=placed,
        out_specs=(P(("group", "dev"), None), P(("group", "dev")), P("dev")),
        check_vma=False,
    )
```

```python
import functools
import jax
import jax.numpy as jnp
from jax import lax
from jax.experimental import pallas as pl
from jax.experimental.pallas import tpu as pltpu
from jax.sharding import PartitionSpec as P

CAP = 160
MESH = pl.DeviceIdType.MESH
NT = (((1,), (1,)), ((), ()))
TN = (((0,), (0,)), ((), ()))
HALF, MID, LOW = 1152, 288, 72
PAIRS = ((0, 0), (1, 0), (1, 1), (2, 0), (2, 1), (2, 2), (3, 0), (3, 1), (3, 2), (3, 3))


def block_starts():
    starts = {}
    for i, j in PAIRS:
        for a in range(2):
            for b in range(2):
                if 2 * j + b <= 2 * i + a:
                    starts[(2 * i + a, 2 * j + b)] = len(starts) * 128
    return starts


STARTS = block_starts()


def vmem():
    return pl.BlockSpec(memory_space=pltpu.VMEM)


def smem():
    return pl.BlockSpec(memory_space=pltpu.SMEM)


def limits():
    return pltpu.CompilerParams(vmem_limit_bytes=48 * 2**20)


def halves(v):
    top = v.astype(jnp.bfloat16)
    return top, (v - top.astype(jnp.float32)).astype(jnp.bfloat16)


def dot(a, b, dims=(((1,), (0,)), ((), ()))):
    return lax.dot_general(a, b, dims, preferred_element_type=jnp.float32)


def narrow(flag):
    return flag.astype(jnp.float32).astype(jnp.bfloat16)


def place_rows(ids, source, table, owners, lists_dev, cap):
    count = ids.shape[1]
    sub = lax.broadcasted_iota(jnp.int32, (table.shape[0], count), 0)
    row_hit = narrow(sub == ids // 128)
    high = dot((table // 256).astype(jnp.float32).astype(jnp.bfloat16), row_hit, TN)
    low = dot((table % 256).astype(jnp.float32).astype(jnp.bfloat16), row_hit, TN)
    lane = lax.broadcasted_iota(jnp.int32, (128, count), 0)
    slot = jnp.sum(jnp.where(lane == ids % 128, high * 256.0 + low, 0.0), axis=0, keepdims=True).astype(jnp.int32)
    owner = slot // lists_dev
    local = slot % lists_dev
    owner_one = narrow(lax.broadcasted_iota(jnp.int32, (owners, count), 0) == owner)
    width = 256
    square = (width, width)
    before = narrow(lax.broadcasted_iota(jnp.int32, square, 0) < lax.broadcasted_iota(jnp.int32, square, 1))
    seen = jnp.zeros((owners, 1), jnp.float32)
    ranks = []
    for k in range(count // width):
        part = owner_one[:, k * width:(k + 1) * width]
        prior = dot(part, before) + seen
        part = part.astype(jnp.float32)
        ranks.append(jnp.sum(prior * part, axis=0, keepdims=True))
        seen = seen + jnp.sum(part, axis=1, keepdims=True)
    rank = jnp.concatenate(ranks, axis=1).astype(jnp.int32)
    rank_hit = lax.broadcasted_iota(jnp.int32, (256, count), 0) == rank

    def collect(value):
        picked = jnp.where(rank_hit, value.astype(jnp.float32), 0.0).astype(jnp.bfloat16)
        return dot(owner_one, picked, NT)

    filled = collect(jnp.ones((1, count), jnp.int32)) > 0.5
    local_at = collect(local // 256) * 256.0 + collect(local % 256)
    source_at = collect(source // 16384) * 16384.0 + collect((source // 128) % 128) * 128.0 + collect(source % 128)
    ids_at = jnp.where(filled, local_at, -1.0).astype(jnp.int32)
    sources_at = jnp.where(filled, source_at, -1.0).astype(jnp.int32)
    return owner * cap + rank, ids_at, sources_at


def front_kernel(lists_dev, cap, x_hbm, list_hbm, source_hbm, table_hbm, tri_ref, pos_ref, got_ref, count_ref,
                 x_ref, list_ref, source_ref, table_ref, load_s, dest, part, core_buf, first_buf, sum_buf, second_buf, mid_sum, tile_buf, tally, tally_buf,
                 core_s, core_r, first_s, first_r, second_s, second_r, tile_s, tile_r, top_s, top_r, odd_s, odd_r,
                 fan_s, fan_r, row_s, row_r, pair_s, pair_r, wide_s, wide_r, id_s, id_r, tally_s, tally_r):
    z = lax.axis_index("group")
    dev = lax.axis_index("dev")
    owners = 32
    x, y, c = dev // 8, (dev // 2) % 4, dev % 2

    def at(xx, yy):
        return (z, (xx * 4 + yy) * 2 + c)

    other = (z, dev + 1 - 2 * c)
    along_x = [at((x + d) % 4, y) for d in (1, 2, 3)]
    along_y = [at(x, (y + d) % 4) for d in (1, 2, 3)]
    along_z = [((z + d) % 8, dev) for d in range(1, 8)]
    barrier = pltpu.get_barrier_semaphore()
    for k in range(1, owners):
        pl.semaphore_signal(barrier, inc=1, device_id=(z, (dev + k) % owners), device_id_type=MESH)
    for peer in along_z:
        pl.semaphore_signal(barrier, inc=1, device_id=peer, device_id_type=MESH)

    loads = [
        pltpu.make_async_copy(list_hbm, list_ref, load_s.at[4]),
        pltpu.make_async_copy(source_hbm, source_ref, load_s.at[5]),
        pltpu.make_async_copy(table_hbm, table_ref, load_s.at[6]),
    ]
    for k in range(4):
        columns = pl.ds(k * 256, 256)
        loads.append(pltpu.make_async_copy(x_hbm.at[:, columns], x_ref.at[:, columns], load_s.at[k]))
    for load in loads[3:] + loads[:3]:
        load.start()
    sent = []

    def copy_to(src, dst, s, r, peer):
        return pltpu.make_async_remote_copy(src_ref=src, dst_ref=dst, send_sem=s, recv_sem=r, device_id=peer,
                                            device_id_type=MESH)

    def send(src, dst, s, r, peer):
        copy = copy_to(src, dst, s, r, peer)
        copy.start()
        sent.append(copy)
        return copy

    def span(start, size):
        return pl.ds(pl.multiple_of(start, 8), size)

    lefts = {}

    def moment(pairs):
        for i, j in pairs:
            if i not in lefts:
                loads[3 + i].wait()
                lefts[i] = x_ref[:, i * 256:(i + 1) * 256].T
            square = dot(lefts[i], x_ref[:, j * 256:(j + 1) * 256])
            for a in range(2):
                for b in range(2):
                    key = (2 * i + a, 2 * j + b)
                    if key in STARTS:
                        begin = STARTS[key]
                        part[begin:begin + 128, :] = square[a * 128:(a + 1) * 128, b * 128:(b + 1) * 128]

    base = [p * 2 * HALF + c * HALF for p in range(2)]
    firsts = [(x, along_x), (y, along_y)]
    seconds = [(y, along_y), (x, along_x)]
    core = [None, None]
    first = [{}, {}]

    def swap(p):
        core[p] = send(part.at[span(p * 2 * HALF + (1 - c) * HALF, HALF)], core_buf.at[p], core_s.at[p], core_r.at[p],
                       other)

    def down_first(p):
        core[p].wait_recv()
        core_buf[p] = core_buf[p] + part[span(base[p], HALF), :]
        f, peers = firsts[p]
        s = seconds[p][0]
        for k in range(4):
            for d in (1, 2, 3):
                begin = ((f + d) % 4) * MID + ((s + 1 + k) % 4) * LOW
                first[p][k, d] = send(core_buf.at[p, span(begin, LOW)], first_buf.at[p, d - 1, k],
                                      first_s.at[p, d - 1, k], first_r.at[p, d - 1, k], peers[d - 1])

    moment(PAIRS[:5])
    pl.semaphore_wait(barrier, 38)
    swap(0)
    moment(PAIRS[5:])
    swap(1)
    down_first(0)
    down_first(1)
    for load in loads[:3]:
        load.wait()
    pos, ids_at, sources_at = place_rows(list_ref[...], source_ref[...], table_ref[...], owners, lists_dev, cap)
    pos_ref[...] = pos
    dest[:, 0, :] = ids_at[:, :128]
    dest[:, 1, :] = ids_at[:, 128:]
    dest[:, 2, :] = sources_at[:, :128]
    dest[:, 3, :] = sources_at[:, 128:]
    second = [{}, {}]
    for k in range(4):
        for p in range(2):
            f = firsts[p][0]
            s, peers = seconds[p]
            for d in (1, 2, 3):
                first[p][k, d].wait_recv()
            own = core_buf[p, span(f * MID + ((s + 1 + k) % 4) * LOW, LOW), :]
            sum_buf[p, k] = (own + first_buf[p, 0, k]) + (first_buf[p, 1, k] + first_buf[p, 2, k])
            if k < 3:
                second[p][k] = send(sum_buf.at[p, k], second_buf.at[p, k], second_s.at[p, k], second_r.at[p, k], peers[k])
    tile = [[], []]
    for p in range(2):
        for k in range(3):
            second[p][k].wait_recv()
        mid_sum[p] = (sum_buf[p, 3] + second_buf[p, 0]) + (second_buf[p, 1] + second_buf[p, 2])
        for d in range(1, 8):
            tile[p].append(send(mid_sum.at[p, span(((z + d) % 8) * 8, 16)], tile_buf.at[p, d - 1],
                                tile_s.at[p, d - 1], tile_r.at[p, d - 1], along_z[d - 1]))
    arrive = []
    for k in range(1, owners):
        peer = (dev + k) % owners
        arrive.append(send(dest.at[peer], got_ref.at[dev], id_s.at[k - 1], id_r.at[k - 1], (z, peer)))
    got_ref[dev] = dest[dev]
    def hand(begin, size, s, r, peer):
        return send(tri_ref.at[span(begin, size)], tri_ref.at[span(begin, size)], s, r, peer)

    top = [[], []]

    def odd(p, d):
        begin = base[p] + firsts[p][0] * MID + seconds[p][0] * LOW + 64
        return copy_to(tri_ref.at[span(begin, 8)], tri_ref.at[span(begin, 8)], odd_s.at[p, d - 1], odd_r.at[p],
                       along_z[d - 1])

    for p in range(2):
        for copy in tile[p]:
            copy.wait_recv()
        total = mid_sum[p, span(z * 8, 16), :]
        for d in range(7):
            total = total + tile_buf[p, d]
        begin = base[p] + firsts[p][0] * MID + seconds[p][0] * LOW
        tri_ref[span(begin + z * 8, 8), :] = total[:8]
        for d in range(1, 8):
            top[p].append(hand(begin + z * 8, 8, top_s.at[p, d - 1], top_r.at[p, d - 1], along_z[d - 1]))

        @pl.when(z == 7)
        def _():
            tri_ref[span(begin + 64, 8), :] = total[8:]
            for d in range(1, 8):
                odd(p, d).start()

    for copy in arrive:
        copy.wait_recv()
    ids = jnp.concatenate([got_ref[:, 0, :], got_ref[:, 1, :]], axis=0)
    ids = jnp.concatenate([ids[k:k + 1, :] for k in range(2 * owners)], axis=1)
    count = ids.shape[1]
    high = lax.broadcasted_iota(jnp.int32, (16, count), 0) == jnp.where(ids >= 0, ids // 128, -1)
    low = lax.broadcasted_iota(jnp.int32, (128, count), 0) == ids % 128
    tally[...] = dot(narrow(high), narrow(low), NT)
    tallies = [send(tally, tally_buf.at[d - 1], tally_s.at[d - 1], tally_r.at[d - 1], along_z[d - 1])
               for d in range(1, 8)]

    fan = [{}, {}]
    row = [{}, {}]
    pair = [[], []]

    def outward(p, k):
        f, peers = firsts[p]
        begin = base[p] + f * MID + ((seconds[p][0] - k + 4) % 4) * LOW
        for d in (1, 2, 3):
            row[p][k, d] = hand(begin, LOW, row_s.at[p, k, d - 1], row_r.at[p, k, d - 1], peers[d - 1])
        pair[p].append(hand(begin, LOW, pair_s.at[p, k], pair_r.at[p, k], other))

    for p in range(2):
        for copy in top[p]:
            copy.wait_recv()

        @pl.when(z != 7)
        def _():
            odd(p, 1).wait_recv()

        s, peers = seconds[p]
        begin = base[p] + firsts[p][0] * MID + s * LOW
        for d in (1, 2, 3):
            fan[p][d] = hand(begin, LOW, fan_s.at[p, d - 1], fan_r.at[p, d - 1], peers[d - 1])
        outward(p, 0)
    for d in (1, 2, 3):
        for p in range(2):
            fan[p][d].wait_recv()
            outward(p, d)
    total = tally[...]
    for d in range(7):
        tallies[d].wait_recv()
        total = total + tally_buf[d]
    count_ref[...] = total.astype(jnp.int32)
    wide = [[], []]
    for d in (1, 2, 3):
        for p in range(2):
            for k in range(4):
                row[p][k, d].wait_recv()
            begin = base[p] + ((firsts[p][0] - d + 4) % 4) * MID
            wide[p].append(hand(begin, MID, wide_s.at[p, d - 1], wide_r.at[p, d - 1], other))
    for p in range(2):
        for copy in pair[p] + wide[p]:
            copy.wait_recv()
    for copy in sent:
        copy.wait_send()

    @pl.when(z == 7)
    def _():
        for p in range(2):
            for d in range(1, 8):
                odd(p, d).wait_send()


def front(corpus_rows, list_ids, source_ids, list_slot, owners, lists_dev, cap):
    count = list_ids.shape[0]
    sem = pltpu.SemaphoreType.DMA
    f32 = jnp.float32
    return pl.pallas_call(
        functools.partial(front_kernel, lists_dev, cap),
        out_shape=(
            jax.ShapeDtypeStruct((4 * HALF, 128), f32),
            jax.ShapeDtypeStruct((1, count), jnp.int32),
            jax.ShapeDtypeStruct((owners, 4, 128), jnp.int32),
            jax.ShapeDtypeStruct((lists_dev // 128, 128), jnp.int32),
        ),
        in_specs=[pl.BlockSpec(memory_space=pl.ANY)] * 4,
        out_specs=(vmem(),) * 4,
        scratch_shapes=[
            pltpu.VMEM(corpus_rows.shape, jnp.bfloat16),
            pltpu.VMEM((1, count), jnp.int32),
            pltpu.VMEM((1, count), jnp.int32),
            pltpu.VMEM((list_slot.shape[0] // 128, 128), jnp.int32),
            sem((7,)),
            pltpu.VMEM((owners, 4, 128), jnp.int32),
            pltpu.VMEM((4 * HALF, 128), f32),
            pltpu.VMEM((2, HALF, 128), f32),
            pltpu.VMEM((2, 3, 4, LOW, 128), f32),
            pltpu.VMEM((2, 4, LOW, 128), f32),
            pltpu.VMEM((2, 3, LOW, 128), f32),
            pltpu.VMEM((2, LOW, 128), f32),
            pltpu.VMEM((2, 7, 16, 128), f32),
            pltpu.VMEM((16, 128), f32),
            pltpu.VMEM((7, 16, 128), f32),
            sem((2,)), sem((2,)), sem((2, 3, 4)), sem((2, 3, 4)), sem((2, 3)), sem((2, 3)), sem((2, 7)), sem((2, 7)),
            sem((2, 7)), sem((2, 7)), sem((2, 7)), sem((2,)), sem((2, 3)), sem((2, 3)), sem((2, 4, 3)), sem((2, 4, 3)),
            sem((2, 4)), sem((2, 4)), sem((2, 3)), sem((2, 3)), sem((31,)), sem((31,)), sem((7,)), sem((7,)),
        ],
        compiler_params=pltpu.CompilerParams(collective_id=0, has_side_effects=True, vmem_limit_bytes=60 * 2**20),
        cost_estimate=pl.CostEstimate(flops=10**10, bytes_accessed=10**8, transcendentals=0),
        name="front",
    )(corpus_rows, list_ids.reshape(1, count), source_ids.reshape(1, count), list_slot.reshape(-1, 128))


def project_kernel(tri_ref, start_ref, x_ref, pos_ref, out_ref, basis_ref, gram_ref, m_hi, m_lo, z_ref):
    eye = lax.broadcasted_iota(jnp.int32, (128, 128), 0) == lax.broadcasted_iota(jnp.int32, (128, 128), 1)
    peak = jnp.zeros((128, 128), jnp.float32)
    for i in range(8):
        for j in range(i + 1):
            at = STARTS[(i, j)]
            block = tri_ref[at:at + 128, :]
            hi, lo = halves(block)
            m_hi[i * 128:(i + 1) * 128, j * 128:(j + 1) * 128] = hi
            m_lo[i * 128:(i + 1) * 128, j * 128:(j + 1) * 128] = lo
            if i != j:
                hi, lo = halves(block.T)
                m_hi[j * 128:(j + 1) * 128, i * 128:(i + 1) * 128] = hi
                m_lo[j * 128:(j + 1) * 128, i * 128:(i + 1) * 128] = lo
            else:
                peak = jnp.maximum(peak, jnp.where(eye, block, 0.0))
    scale = 1.0 / jnp.max(jnp.max(peak, axis=0, keepdims=True), axis=1, keepdims=True)
    width = start_ref.shape[1]

    def times_moment(v):
        hi, lo = halves(v * scale)
        both = dot(m_hi[...], jnp.concatenate([hi, lo], axis=1))
        return (both[:, :width] + both[:, width:]) + dot(m_lo[...], hi)

    product = times_moment(times_moment(start_ref[...]))
    product = product * lax.rsqrt(jnp.sum(product * product, axis=0, keepdims=True))
    hi, lo = halves(product)
    basis_ref[:, :width] = hi
    basis_ref[:, width:] = lo
    cross = dot(hi, basis_ref[...], TN)
    mixed = cross[:, width:]
    gram_ref[...] = cross[:, :width] + (mixed + mixed.T)
    step = 256

    @pl.loop(0, x_ref.shape[0] // step)
    def _(k):
        at = pl.ds(pl.multiple_of(k * step, step), step)
        both = dot(x_ref[at, :], basis_ref[...])
        code = both[:, :width] + both[:, width:]
        z_ref[at, 0, :] = code[:, :128]
        z_ref[at, 1, :] = code[:, 128:]

    @pl.loop(0, x_ref.shape[0] // 16)
    def _(k):
        for u in range(16):
            out_ref[pos_ref[0, k * 16 + u]] = z_ref[k * 16 + u]


def project(tri, start, x, pos, slots):
    feature, width = start.shape
    return pl.pallas_call(
        project_kernel,
        out_shape=(
            jax.ShapeDtypeStruct((slots, 2, width // 2), jnp.float32),
            jax.ShapeDtypeStruct((feature, 2 * width), jnp.bfloat16),
            jax.ShapeDtypeStruct((width, width), jnp.float32),
        ),
        in_specs=[vmem(), vmem(), vmem(), smem()],
        out_specs=(vmem(), vmem(), vmem()),
        scratch_shapes=[
            pltpu.VMEM((feature, feature), jnp.bfloat16),
            pltpu.VMEM((feature, feature), jnp.bfloat16),
            pltpu.VMEM((x.shape[0], 2, width // 2), jnp.float32),
        ],
        compiler_params=limits(),
        cost_estimate=pl.CostEstimate(flops=10**10, bytes_accessed=2 * 10**7, transcendentals=0),
        name="project",
    )(tri, start, x, pos)


def factor_kernel(gram_ref, inverse_ref, pivot_ref, aug):
    size = gram_ref.shape[0]
    block = 32
    panel = 8
    aug[:, :size] = gram_ref[...]
    aug[:, size:] = (
        lax.broadcasted_iota(jnp.int32, (size, size), 0) == lax.broadcasted_iota(jnp.int32, (size, size), 1)
    ).astype(jnp.float32)
    row_at = lax.broadcasted_iota(jnp.int32, (block, 128), 0)
    lane_at = lax.broadcasted_iota(jnp.int32, (block, 128), 1)
    least = jnp.full((1, 128), 1e30, jnp.float32)
    for b in range(size // block):
        lo, hi = b * block, (b + 1) * block
        square = aug[lo:hi, lo:hi]
        unit = (row_at[:, :block] == lane_at[:, :block]).astype(jnp.float32)
        work = jnp.concatenate([square, unit, jnp.zeros((block, 128 - 2 * block), jnp.float32)], axis=1)
        for p in range(block // panel):
            cols = [
                jnp.broadcast_to(work[:, p * panel + j:p * panel + j + 1], (block, 128)) for j in range(panel)
            ]
            for j in range(panel):
                k = p * panel + j
                pivot = cols[j][k:k + 1, :]
                least = jnp.minimum(least, pivot)
                root = lax.rsqrt(pivot)
                column = jnp.where(row_at > k, cols[j] * root, 0.0)
                for jj in range(j + 1, panel):
                    kk = p * panel + jj
                    cols[jj] = cols[jj] - column * column[kk:kk + 1, :]
                row = work[k:k + 1, :] * root
                work = jnp.where(row_at == k, row, work - column * row)
        inverse = work[:, block:2 * block]
        rows = lax.dot_general(inverse, aug[lo:hi, :], (((1,), (0,)), ((), ())), precision=lax.Precision.HIGHEST,
                               preferred_element_type=jnp.float32)
        aug[lo:hi, :] = rows
        if hi < size:
            below = rows[:, hi:size].T
            aug[hi:, :] -= lax.dot_general(below, rows, (((1,), (0,)), ((), ())), precision=lax.Precision.HIGHEST,
                                           preferred_element_type=jnp.float32)
    whole = aug[:, size:].T
    top, bottom = halves(whole)
    inverse_ref[:, :size] = top
    inverse_ref[:, size:] = bottom
    pivot_ref[...] = least


def factor(gram):
    size = gram.shape[0]
    return pl.pallas_call(
        factor_kernel,
        out_shape=(
            jax.ShapeDtypeStruct((size, 2 * size), jnp.bfloat16),
            jax.ShapeDtypeStruct((1, 128), jnp.float32),
        ),
        in_specs=[vmem()],
        out_specs=(vmem(), vmem()),
        scratch_shapes=[pltpu.VMEM((size, 2 * size), jnp.float32)],
        compiler_params=limits(),
        cost_estimate=pl.CostEstimate(flops=10**9, bytes_accessed=10**7, transcendentals=0),
        name="factor",
    )(gram)


def offset_kernel(c_ref, basis_ref, id_ref, out_ref, z_ref):
    width = basis_ref.shape[1] // 2
    step = 256

    @pl.loop(0, c_ref.shape[0] // step)
    def _(k):
        at = pl.ds(pl.multiple_of(k * step, step), step)
        both = dot(c_ref[at, :], basis_ref[...])
        code = both[:, :width] + both[:, width:]
        z_ref[at, 0, :] = code[:, :128]
        z_ref[at, 1, :] = code[:, 128:]

    @pl.loop(0, out_ref.shape[0] // 16)
    def _(k):
        for u in range(16):
            out_ref[k * 16 + u] = z_ref[jnp.maximum(id_ref[k * 16 + u], 0)]


def offsets_at(centroids, basis, ids):
    width = basis.shape[1] // 2
    return pl.pallas_call(
        offset_kernel,
        out_shape=jax.ShapeDtypeStruct((ids.shape[0], 2, width // 2), jnp.float32),
        in_specs=[vmem(), vmem(), smem()],
        out_specs=vmem(),
        scratch_shapes=[pltpu.VMEM((centroids.shape[0], 2, width // 2), jnp.float32)],
        compiler_params=limits(),
        cost_estimate=pl.CostEstimate(flops=10**10, bytes_accessed=10**7, transcendentals=0),
        name="offsets",
    )(centroids, basis, ids)


def finish_kernel(senders, z_ref, off_ref, count_ref, inverse_ref, out_ref):
    width = out_ref.shape[1]
    cap = z_ref.shape[0] // senders
    low = z_ref[:, 0, :] - off_ref[:, 0, :]
    high = z_ref[:, 1, :] - off_ref[:, 1, :]
    hi, lo = halves(jnp.concatenate([low, high], axis=1))
    both = dot(hi, inverse_ref[...])
    code = (both[:, :width] + both[:, width:]) + dot(lo, inverse_ref[:, :width])
    rank = lax.broadcasted_iota(jnp.int32, (cap, width), 0)
    for s in range(senders):
        filled = rank < count_ref[pl.program_id(0) * senders + s]
        part = slice(s * cap, (s + 1) * cap)
        out_ref[part, :] = jnp.where(filled, code[part, :], 0.0).astype(jnp.bfloat16)


def finish(z, off, filled, inverse):
    slots = z.shape[0]
    width = inverse.shape[0]
    senders = 4
    step = senders * (slots // filled.shape[0])
    return pl.pallas_call(
        functools.partial(finish_kernel, senders),
        out_shape=jax.ShapeDtypeStruct((slots, width), jnp.bfloat16),
        grid=(slots // step,),
        in_specs=[
            pl.BlockSpec((step, 2, width // 2), lambda s: (s, 0, 0)),
            pl.BlockSpec((step, 2, width // 2), lambda s: (s, 0, 0)),
            smem(),
            pl.BlockSpec((width, 2 * width), lambda s: (0, 0)),
        ],
        out_specs=pl.BlockSpec((step, width), lambda s: (s, 0)),
        compiler_params=limits(),
        cost_estimate=pl.CostEstimate(flops=2 * 10**9, bytes_accessed=13 * 10**6, transcendentals=0),
        name="finish",
    )(z, off, filled, inverse)


exact_mode = lax.Precision.HIGHEST
PIVOT_LEAST = 1.0 / 64.0


def orthonormal(product):
    gram_matrix = jnp.dot(product.T, product, precision=exact_mode, preferred_element_type=jnp.float32)
    lower = jnp.linalg.cholesky(gram_matrix)
    return jax.scipy.linalg.solve_triangular(lower, product.T, lower=True).T


def careful(tri, start, x, centroids, pos, ids):
    owners = lax.axis_size("dev")
    slots = ids.shape[0]
    grid = [[None] * 8 for _ in range(8)]
    for i in range(8):
        for j in range(i + 1):
            at = STARTS[(i, j)]
            grid[i][j] = tri[at:at + 128]
            grid[j][i] = tri[at:at + 128].T
    moment = jnp.block(grid)
    basis = start
    for sweep in range(2):
        product = jnp.dot(moment, basis, precision=exact_mode, preferred_element_type=jnp.float32)
        basis = orthonormal(product)
    width = start.shape[1]
    projected = jnp.dot(x, basis, precision=exact_mode, preferred_element_type=jnp.float32)
    sent = jnp.zeros((slots, width), jnp.float32).at[pos.reshape(-1)].set(projected)
    sent = sent.reshape(owners, slots // owners, width)
    values = lax.all_to_all(sent, "dev", split_axis=0, concat_axis=0, tiled=True).reshape(slots, width)
    offsets = jnp.dot(centroids, basis, precision=exact_mode, preferred_element_type=jnp.float32)
    code = values - jnp.take(offsets, jnp.maximum(ids, 0), axis=0)
    return jnp.where(ids[:, None] >= 0, code, 0.0).astype(jnp.bfloat16)


def shards(corpus_rows, list_ids, source_ids, list_slot, centroids, start_basis):
    owners = lax.axis_size("dev")
    lists_dev = centroids.shape[0]
    slots = owners * CAP
    tri, pos, arrived, counts = front(corpus_rows, list_ids, source_ids, list_slot, owners, lists_dev, CAP)
    sent, basis, gram = project(tri, start_basis, corpus_rows, pos, slots)
    half = start_basis.shape[1] // 2
    values = lax.all_to_all(
        sent.reshape(owners, CAP, 2, half), "dev", split_axis=0, concat_axis=0, tiled=True
    ).reshape(slots, 2, half)
    ids = arrived[:, :2].reshape(owners, 256)[:, :CAP]
    filled = jnp.sum((ids >= 0).astype(jnp.int32), axis=1)
    ids = ids.reshape(slots)
    row_sources = arrived[:, 2:].reshape(owners, 256)[:, :CAP].reshape(slots)
    inverse, pivots = factor(gram)
    off = offsets_at(centroids, basis, ids)
    row_codes = lax.cond(
        jnp.min(pivots) >= PIVOT_LEAST,
        lambda: finish(values, off, filled, inverse),
        lambda: careful(tri, start_basis, corpus_rows, centroids, pos, ids),
    )
    return row_codes, row_sources, counts.reshape(lists_dev)


def solution(mesh):
    placed = (
        P(("group", "dev"), None),
        P(("group", "dev")),
        P(("group", "dev")),
        P(),
        P("dev", None),
        P(),
    )
    return jax.shard_map(
        shards,
        mesh=mesh,
        in_specs=placed,
        out_specs=(P(("group", "dev"), None), P(("group", "dev")), P("dev")),
        check_vma=False,
    )
```

```python
import functools
import jax
import jax.numpy as jnp
from jax import lax
from jax.experimental import pallas as pl
from jax.experimental.pallas import tpu as pltpu
from jax.sharding import PartitionSpec as P

CAP = 160
MESH = pl.DeviceIdType.MESH
NT = (((1,), (1,)), ((), ()))
TN = (((0,), (0,)), ((), ()))
HALF, MID, LOW = 1152, 288, 72
PAIRS = ((0, 0), (1, 0), (1, 1), (2, 0), (2, 1), (2, 2), (3, 0), (3, 1), (3, 2), (3, 3))


def block_starts():
    starts = {}
    for i, j in PAIRS:
        for a in range(2):
            for b in range(2):
                if 2 * j + b <= 2 * i + a:
                    starts[(2 * i + a, 2 * j + b)] = len(starts) * 128
    return starts


STARTS = block_starts()


def vmem():
    return pl.BlockSpec(memory_space=pltpu.VMEM)


def smem():
    return pl.BlockSpec(memory_space=pltpu.SMEM)


def limits():
    return pltpu.CompilerParams(vmem_limit_bytes=48 * 2**20)


def halves(v):
    top = v.astype(jnp.bfloat16)
    return top, (v - top.astype(jnp.float32)).astype(jnp.bfloat16)


def dot(a, b, dims=(((1,), (0,)), ((), ()))):
    return lax.dot_general(a, b, dims, preferred_element_type=jnp.float32)


def narrow(flag):
    return flag.astype(jnp.float32).astype(jnp.bfloat16)


def place_rows(ids, source, table, owners, lists_dev, cap):
    count = ids.shape[1]
    sub = lax.broadcasted_iota(jnp.int32, (table.shape[0], count), 0)
    row_hit = narrow(sub == ids // 128)
    high = dot((table // 256).astype(jnp.float32).astype(jnp.bfloat16), row_hit, TN)
    low = dot((table % 256).astype(jnp.float32).astype(jnp.bfloat16), row_hit, TN)
    lane = lax.broadcasted_iota(jnp.int32, (128, count), 0)
    slot = jnp.sum(jnp.where(lane == ids % 128, high * 256.0 + low, 0.0), axis=0, keepdims=True).astype(jnp.int32)
    owner = slot // lists_dev
    local = slot % lists_dev
    owner_one = narrow(lax.broadcasted_iota(jnp.int32, (owners, count), 0) == owner)
    width = 256
    square = (width, width)
    before = narrow(lax.broadcasted_iota(jnp.int32, square, 0) < lax.broadcasted_iota(jnp.int32, square, 1))
    seen = jnp.zeros((owners, 1), jnp.float32)
    ranks = []
    for k in range(count // width):
        part = owner_one[:, k * width:(k + 1) * width]
        prior = dot(part, before) + seen
        part = part.astype(jnp.float32)
        ranks.append(jnp.sum(prior * part, axis=0, keepdims=True))
        seen = seen + jnp.sum(part, axis=1, keepdims=True)
    rank = jnp.concatenate(ranks, axis=1).astype(jnp.int32)
    rank_hit = lax.broadcasted_iota(jnp.int32, (256, count), 0) == rank

    def collect(value):
        picked = jnp.where(rank_hit, value.astype(jnp.float32), 0.0).astype(jnp.bfloat16)
        return dot(owner_one, picked, NT)

    filled = collect(jnp.ones((1, count), jnp.int32)) > 0.5
    local_at = collect(local // 256) * 256.0 + collect(local % 256)
    source_at = collect(source // 16384) * 16384.0 + collect((source // 128) % 128) * 128.0 + collect(source % 128)
    ids_at = jnp.where(filled, local_at, -1.0).astype(jnp.int32)
    sources_at = jnp.where(filled, source_at, -1.0).astype(jnp.int32)
    return owner * (2 * cap) + rank, ids_at, sources_at


def front_kernel(lists_dev, cap, x_hbm, list_hbm, source_hbm, table_hbm, tri_ref, pos_ref, got_ref, count_ref,
                 x_ref, list_ref, source_ref, table_ref, load_s, dest, part, core_buf, first_buf, sum_buf, second_buf, mid_sum, tile_buf, tally, tally_buf,
                 core_s, core_r, first_s, first_r, second_s, second_r, tile_s, tile_r, top_s, top_r, odd_s, odd_r,
                 fan_s, fan_r, row_s, row_r, pair_s, pair_r, wide_s, wide_r, id_s, id_r, tally_s, tally_r):
    z = lax.axis_index("group")
    dev = lax.axis_index("dev")
    owners = 32
    x, y, c = dev // 8, (dev // 2) % 4, dev % 2

    def at(xx, yy):
        return (z, (xx * 4 + yy) * 2 + c)

    other = (z, dev + 1 - 2 * c)
    along_x = [at((x + d) % 4, y) for d in (1, 2, 3)]
    along_y = [at(x, (y + d) % 4) for d in (1, 2, 3)]
    along_z = [((z + d) % 8, dev) for d in range(1, 8)]
    barrier = pltpu.get_barrier_semaphore()
    for k in range(1, owners):
        pl.semaphore_signal(barrier, inc=1, device_id=(z, (dev + k) % owners), device_id_type=MESH)
    for peer in along_z:
        pl.semaphore_signal(barrier, inc=1, device_id=peer, device_id_type=MESH)

    loads = [
        pltpu.make_async_copy(list_hbm, list_ref, load_s.at[4]),
        pltpu.make_async_copy(source_hbm, source_ref, load_s.at[5]),
        pltpu.make_async_copy(table_hbm, table_ref, load_s.at[6]),
    ]
    for k in range(4):
        columns = pl.ds(k * 256, 256)
        loads.append(pltpu.make_async_copy(x_hbm.at[:, columns], x_ref.at[:, columns], load_s.at[k]))
    for load in loads[3:] + loads[:3]:
        load.start()
    sent = []

    def copy_to(src, dst, s, r, peer):
        return pltpu.make_async_remote_copy(src_ref=src, dst_ref=dst, send_sem=s, recv_sem=r, device_id=peer,
                                            device_id_type=MESH)

    def send(src, dst, s, r, peer):
        copy = copy_to(src, dst, s, r, peer)
        copy.start()
        sent.append(copy)
        return copy

    def span(start, size):
        return pl.ds(pl.multiple_of(start, 8), size)

    lefts = {}

    def moment(pairs):
        for i, j in pairs:
            if i not in lefts:
                loads[3 + i].wait()
                lefts[i] = x_ref[:, i * 256:(i + 1) * 256].T
            square = dot(lefts[i], x_ref[:, j * 256:(j + 1) * 256])
            for a in range(2):
                for b in range(2):
                    key = (2 * i + a, 2 * j + b)
                    if key in STARTS:
                        begin = STARTS[key]
                        part[begin:begin + 128, :] = square[a * 128:(a + 1) * 128, b * 128:(b + 1) * 128]

    base = [p * 2 * HALF + c * HALF for p in range(2)]
    firsts = [(x, along_x), (y, along_y)]
    seconds = [(y, along_y), (x, along_x)]
    core = [None, None]
    first = [{}, {}]

    def swap(p):
        core[p] = send(part.at[span(p * 2 * HALF + (1 - c) * HALF, HALF)], core_buf.at[p], core_s.at[p], core_r.at[p],
                       other)

    def down_first(p):
        core[p].wait_recv()
        core_buf[p] = core_buf[p] + part[span(base[p], HALF), :]
        f, peers = firsts[p]
        s = seconds[p][0]
        for k in range(4):
            for d in (1, 2, 3):
                begin = ((f + d) % 4) * MID + ((s + 1 + k) % 4) * LOW
                first[p][k, d] = send(core_buf.at[p, span(begin, LOW)], first_buf.at[p, d - 1, k],
                                      first_s.at[p, d - 1, k], first_r.at[p, d - 1, k], peers[d - 1])

    moment(PAIRS[:5])
    pl.semaphore_wait(barrier, 38)
    swap(0)
    moment(PAIRS[5:])
    swap(1)
    down_first(0)
    down_first(1)
    for load in loads[:3]:
        load.wait()
    pos, ids_at, sources_at = place_rows(list_ref[...], source_ref[...], table_ref[...], owners, lists_dev, cap)
    pos_ref[...] = pos
    dest[:, 0, :] = ids_at[:, :128]
    dest[:, 1, :] = ids_at[:, 128:]
    dest[:, 2, :] = sources_at[:, :128]
    dest[:, 3, :] = sources_at[:, 128:]
    second = [{}, {}]
    for k in range(4):
        for p in range(2):
            f = firsts[p][0]
            s, peers = seconds[p]
            for d in (1, 2, 3):
                first[p][k, d].wait_recv()
            own = core_buf[p, span(f * MID + ((s + 1 + k) % 4) * LOW, LOW), :]
            sum_buf[p, k] = (own + first_buf[p, 0, k]) + (first_buf[p, 1, k] + first_buf[p, 2, k])
            if k < 3:
                second[p][k] = send(sum_buf.at[p, k], second_buf.at[p, k], second_s.at[p, k], second_r.at[p, k], peers[k])
    tile = [[], []]
    for p in range(2):
        for k in range(3):
            second[p][k].wait_recv()
        mid_sum[p] = (sum_buf[p, 3] + second_buf[p, 0]) + (second_buf[p, 1] + second_buf[p, 2])
        for d in range(1, 8):
            tile[p].append(send(mid_sum.at[p, span(((z + d) % 8) * 8, 16)], tile_buf.at[p, d - 1],
                                tile_s.at[p, d - 1], tile_r.at[p, d - 1], along_z[d - 1]))
    arrive = []
    for k in range(1, owners):
        peer = (dev + k) % owners
        arrive.append(send(dest.at[peer], got_ref.at[dev], id_s.at[k - 1], id_r.at[k - 1], (z, peer)))
    got_ref[dev] = dest[dev]
    def hand(begin, size, s, r, peer):
        return send(tri_ref.at[span(begin, size)], tri_ref.at[span(begin, size)], s, r, peer)

    top = [[], []]

    def odd(p, d):
        begin = base[p] + firsts[p][0] * MID + seconds[p][0] * LOW + 64
        return copy_to(tri_ref.at[span(begin, 8)], tri_ref.at[span(begin, 8)], odd_s.at[p, d - 1], odd_r.at[p],
                       along_z[d - 1])

    for p in range(2):
        for copy in tile[p]:
            copy.wait_recv()
        total = mid_sum[p, span(z * 8, 16), :]
        for d in range(7):
            total = total + tile_buf[p, d]
        begin = base[p] + firsts[p][0] * MID + seconds[p][0] * LOW
        tri_ref[span(begin + z * 8, 8), :] = total[:8]
        for d in range(1, 8):
            top[p].append(hand(begin + z * 8, 8, top_s.at[p, d - 1], top_r.at[p, d - 1], along_z[d - 1]))

        @pl.when(z == 7)
        def _():
            tri_ref[span(begin + 64, 8), :] = total[8:]
            for d in range(1, 8):
                odd(p, d).start()

    for copy in arrive:
        copy.wait_recv()
    ids = jnp.concatenate([got_ref[:, 0, :], got_ref[:, 1, :]], axis=0)
    ids = jnp.concatenate([ids[k:k + 1, :] for k in range(2 * owners)], axis=1)
    count = ids.shape[1]
    high = lax.broadcasted_iota(jnp.int32, (16, count), 0) == jnp.where(ids >= 0, ids // 128, -1)
    low = lax.broadcasted_iota(jnp.int32, (128, count), 0) == ids % 128
    tally[...] = dot(narrow(high), narrow(low), NT)
    tallies = [send(tally, tally_buf.at[d - 1], tally_s.at[d - 1], tally_r.at[d - 1], along_z[d - 1])
               for d in range(1, 8)]

    fan = [{}, {}]
    row = [{}, {}]
    pair = [[], []]

    def outward(p, k):
        f, peers = firsts[p]
        begin = base[p] + f * MID + ((seconds[p][0] - k + 4) % 4) * LOW
        for d in (1, 2, 3):
            row[p][k, d] = hand(begin, LOW, row_s.at[p, k, d - 1], row_r.at[p, k, d - 1], peers[d - 1])
        pair[p].append(hand(begin, LOW, pair_s.at[p, k], pair_r.at[p, k], other))

    for p in range(2):
        for copy in top[p]:
            copy.wait_recv()

        @pl.when(z != 7)
        def _():
            odd(p, 1).wait_recv()

        s, peers = seconds[p]
        begin = base[p] + firsts[p][0] * MID + s * LOW
        for d in (1, 2, 3):
            fan[p][d] = hand(begin, LOW, fan_s.at[p, d - 1], fan_r.at[p, d - 1], peers[d - 1])
        outward(p, 0)
    for d in (1, 2, 3):
        for p in range(2):
            fan[p][d].wait_recv()
            outward(p, d)
    total = tally[...]
    for d in range(7):
        tallies[d].wait_recv()
        total = total + tally_buf[d]
    count_ref[...] = total.astype(jnp.int32)
    wide = [[], []]
    for d in (1, 2, 3):
        for p in range(2):
            for k in range(4):
                row[p][k, d].wait_recv()
            begin = base[p] + ((firsts[p][0] - d + 4) % 4) * MID
            wide[p].append(hand(begin, MID, wide_s.at[p, d - 1], wide_r.at[p, d - 1], other))
    for p in range(2):
        for copy in pair[p] + wide[p]:
            copy.wait_recv()
    for copy in sent:
        copy.wait_send()

    @pl.when(z == 7)
    def _():
        for p in range(2):
            for d in range(1, 8):
                odd(p, d).wait_send()


def front(corpus_rows, list_ids, source_ids, list_slot, owners, lists_dev, cap):
    count = list_ids.shape[0]
    sem = pltpu.SemaphoreType.DMA
    f32 = jnp.float32
    return pl.pallas_call(
        functools.partial(front_kernel, lists_dev, cap),
        out_shape=(
            jax.ShapeDtypeStruct((4 * HALF, 128), f32),
            jax.ShapeDtypeStruct((1, count), jnp.int32),
            jax.ShapeDtypeStruct((owners, 4, 128), jnp.int32),
            jax.ShapeDtypeStruct((lists_dev // 128, 128), jnp.int32),
        ),
        in_specs=[pl.BlockSpec(memory_space=pl.ANY)] * 4,
        out_specs=(vmem(),) * 4,
        scratch_shapes=[
            pltpu.VMEM(corpus_rows.shape, jnp.bfloat16),
            pltpu.VMEM((1, count), jnp.int32),
            pltpu.VMEM((1, count), jnp.int32),
            pltpu.VMEM((list_slot.shape[0] // 128, 128), jnp.int32),
            sem((7,)),
            pltpu.VMEM((owners, 4, 128), jnp.int32),
            pltpu.VMEM((4 * HALF, 128), f32),
            pltpu.VMEM((2, HALF, 128), f32),
            pltpu.VMEM((2, 3, 4, LOW, 128), f32),
            pltpu.VMEM((2, 4, LOW, 128), f32),
            pltpu.VMEM((2, 3, LOW, 128), f32),
            pltpu.VMEM((2, LOW, 128), f32),
            pltpu.VMEM((2, 7, 16, 128), f32),
            pltpu.VMEM((16, 128), f32),
            pltpu.VMEM((7, 16, 128), f32),
            sem((2,)), sem((2,)), sem((2, 3, 4)), sem((2, 3, 4)), sem((2, 3)), sem((2, 3)), sem((2, 7)), sem((2, 7)),
            sem((2, 7)), sem((2, 7)), sem((2, 7)), sem((2,)), sem((2, 3)), sem((2, 3)), sem((2, 4, 3)), sem((2, 4, 3)),
            sem((2, 4)), sem((2, 4)), sem((2, 3)), sem((2, 3)), sem((31,)), sem((31,)), sem((7,)), sem((7,)),
        ],
        compiler_params=pltpu.CompilerParams(collective_id=0, has_side_effects=True, vmem_limit_bytes=60 * 2**20),
        cost_estimate=pl.CostEstimate(flops=10**10, bytes_accessed=10**8, transcendentals=0),
        name="front",
    )(corpus_rows, list_ids.reshape(1, count), source_ids.reshape(1, count), list_slot.reshape(-1, 128))


def project_rows(rows_ref, basis_ref, z_ref):
    count = rows_ref.shape[0]
    width = basis_ref.shape[1] // 2
    step = 1024
    for begin in range(0, count, step):
        both = dot(rows_ref[begin:begin + step, :], basis_ref[...])
        code = both[:, :width] + both[:, width:]
        z_ref[begin:begin + step, :] = code[:, :128]
        z_ref[count + begin:count + begin + step, :] = code[:, 128:]


def project_kernel(cap, tri_ref, start_ref, x_hbm, pos_ref, out_ref, basis_ref, gram_ref, x_ref, load_s, m_hi, m_lo,
                   z_ref):
    load = pltpu.make_async_copy(x_hbm, x_ref, load_s)
    load.start()
    eye = lax.broadcasted_iota(jnp.int32, (128, 128), 0) == lax.broadcasted_iota(jnp.int32, (128, 128), 1)
    peak = jnp.zeros((128, 128), jnp.float32)
    for i in range(8):
        for j in range(i + 1):
            at = STARTS[(i, j)]
            block = tri_ref[at:at + 128, :]
            hi, lo = halves(block)
            m_hi[i * 128:(i + 1) * 128, j * 128:(j + 1) * 128] = hi
            m_lo[i * 128:(i + 1) * 128, j * 128:(j + 1) * 128] = lo
            if i != j:
                hi, lo = halves(block.T)
                m_hi[j * 128:(j + 1) * 128, i * 128:(i + 1) * 128] = hi
                m_lo[j * 128:(j + 1) * 128, i * 128:(i + 1) * 128] = lo
            else:
                peak = jnp.maximum(peak, jnp.where(eye, block, 0.0))
    scale = 1.0 / jnp.max(jnp.max(peak, axis=0, keepdims=True), axis=1, keepdims=True)
    width = start_ref.shape[1]

    def times_moment(v):
        hi, lo = halves(v * scale)
        both = dot(m_hi[...], jnp.concatenate([hi, lo], axis=1))
        return (both[:, :width] + both[:, width:]) + dot(m_lo[...], hi)

    product = times_moment(times_moment(start_ref[...]))
    product = product * lax.rsqrt(jnp.sum(product * product, axis=0, keepdims=True))
    hi, lo = halves(product)
    basis_ref[:, :width] = hi
    basis_ref[:, width:] = lo
    cross = dot(hi, basis_ref[...], TN)
    mixed = cross[:, width:]
    gram_ref[...] = cross[:, :width] + (mixed + mixed.T)
    load.wait()
    project_rows(x_ref, basis_ref, z_ref)
    count = x_ref.shape[0]

    @pl.loop(0, count // 16)
    def _(k):
        for u in range(16):
            row = k * 16 + u
            slot = pos_ref[0, row]
            out_ref[pl.ds(slot, 1), :] = z_ref[pl.ds(row, 1), :]
            out_ref[pl.ds(slot + cap, 1), :] = z_ref[pl.ds(row + count, 1), :]


def project(tri, start, x, pos, owners, cap):
    feature, width = start.shape
    return pl.pallas_call(
        functools.partial(project_kernel, cap),
        out_shape=(
            jax.ShapeDtypeStruct((owners * 2 * cap, 128), jnp.float32),
            jax.ShapeDtypeStruct((feature, 2 * width), jnp.bfloat16),
            jax.ShapeDtypeStruct((width, width), jnp.float32),
        ),
        in_specs=[vmem(), vmem(), pl.BlockSpec(memory_space=pl.ANY), smem()],
        out_specs=(vmem(), vmem(), vmem()),
        scratch_shapes=[
            pltpu.VMEM(x.shape, jnp.bfloat16),
            pltpu.SemaphoreType.DMA,
            pltpu.VMEM((feature, feature), jnp.bfloat16),
            pltpu.VMEM((feature, feature), jnp.bfloat16),
            pltpu.VMEM((2 * x.shape[0], 128), jnp.float32),
        ],
        compiler_params=limits(),
        cost_estimate=pl.CostEstimate(flops=10**10, bytes_accessed=2 * 10**7, transcendentals=0),
        name="project",
    )(tri, start, x, pos)


def factor_kernel(gram_ref, inverse_ref, pivot_ref, aug):
    size = gram_ref.shape[0]
    block = 32
    panel = 8
    aug[:, :size] = gram_ref[...]
    aug[:, size:] = (
        lax.broadcasted_iota(jnp.int32, (size, size), 0) == lax.broadcasted_iota(jnp.int32, (size, size), 1)
    ).astype(jnp.float32)
    row_at = lax.broadcasted_iota(jnp.int32, (block, 128), 0)
    lane_at = lax.broadcasted_iota(jnp.int32, (block, 128), 1)
    least = jnp.full((1, 128), 1e30, jnp.float32)
    for b in range(size // block):
        lo, hi = b * block, (b + 1) * block
        square = aug[lo:hi, lo:hi]
        unit = (row_at[:, :block] == lane_at[:, :block]).astype(jnp.float32)
        work = jnp.concatenate([square, unit, jnp.zeros((block, 128 - 2 * block), jnp.float32)], axis=1)
        for p in range(block // panel):
            cols = [
                jnp.broadcast_to(work[:, p * panel + j:p * panel + j + 1], (block, 128)) for j in range(panel)
            ]
            for j in range(panel):
                k = p * panel + j
                pivot = cols[j][k:k + 1, :]
                least = jnp.minimum(least, pivot)
                root = lax.rsqrt(pivot)
                column = jnp.where(row_at > k, cols[j] * root, 0.0)
                for jj in range(j + 1, panel):
                    kk = p * panel + jj
                    cols[jj] = cols[jj] - column * column[kk:kk + 1, :]
                row = work[k:k + 1, :] * root
                work = jnp.where(row_at == k, row, work - column * row)
        inverse = work[:, block:2 * block]
        rows = lax.dot_general(inverse, aug[lo:hi, :], (((1,), (0,)), ((), ())), precision=lax.Precision.HIGHEST,
                               preferred_element_type=jnp.float32)
        aug[lo:hi, :] = rows
        if hi < size:
            below = rows[:, hi:size].T
            aug[hi:, :] -= lax.dot_general(below, rows, (((1,), (0,)), ((), ())), precision=lax.Precision.HIGHEST,
                                           preferred_element_type=jnp.float32)
    whole = aug[:, size:].T
    top, bottom = halves(whole)
    inverse_ref[:, :size] = top
    inverse_ref[:, size:] = bottom
    pivot_ref[...] = least


def factor(gram):
    size = gram.shape[0]
    return pl.pallas_call(
        factor_kernel,
        out_shape=(
            jax.ShapeDtypeStruct((size, 2 * size), jnp.bfloat16),
            jax.ShapeDtypeStruct((1, 128), jnp.float32),
        ),
        in_specs=[vmem()],
        out_specs=(vmem(), vmem()),
        scratch_shapes=[pltpu.VMEM((size, 2 * size), jnp.float32)],
        compiler_params=limits(),
        cost_estimate=pl.CostEstimate(flops=10**9, bytes_accessed=10**7, transcendentals=0),
        name="factor",
    )(gram)


def offset_kernel(cap, c_ref, basis_ref, id_ref, out_ref, z_ref):
    project_rows(c_ref, basis_ref, z_ref)
    count = c_ref.shape[0]

    @pl.loop(0, id_ref.shape[0] // cap)
    def _(sender):
        @pl.loop(0, cap // 16)
        def _(k):
            for u in range(16):
                rank = k * 16 + u
                row = jnp.maximum(id_ref[sender * cap + rank], 0)
                slot = sender * (2 * cap) + rank
                out_ref[pl.ds(slot, 1), :] = z_ref[pl.ds(row, 1), :]
                out_ref[pl.ds(slot + cap, 1), :] = z_ref[pl.ds(row + count, 1), :]


def offsets_at(centroids, basis, ids, cap):
    return pl.pallas_call(
        functools.partial(offset_kernel, cap),
        out_shape=jax.ShapeDtypeStruct((2 * ids.shape[0], 128), jnp.float32),
        in_specs=[vmem(), vmem(), smem()],
        out_specs=vmem(),
        scratch_shapes=[pltpu.VMEM((2 * centroids.shape[0], 128), jnp.float32)],
        compiler_params=limits(),
        cost_estimate=pl.CostEstimate(flops=10**10, bytes_accessed=10**7, transcendentals=0),
        name="offsets",
    )(centroids, basis, ids)


def finish_kernel(senders, z_ref, off_ref, count_ref, inverse_ref, out_ref):
    width = out_ref.shape[1]
    cap = out_ref.shape[0] // senders
    rank = lax.broadcasted_iota(jnp.int32, (cap, width), 0)
    for s in range(senders):
        begin = 2 * s * cap
        gap = z_ref[begin:begin + 2 * cap, :] - off_ref[begin:begin + 2 * cap, :]
        hi, lo = halves(jnp.concatenate([gap[:cap], gap[cap:]], axis=1))
        both = dot(hi, inverse_ref[...])
        code = (both[:, :width] + both[:, width:]) + dot(lo, inverse_ref[:, :width])
        filled = rank < count_ref[pl.program_id(0) * senders + s]
        out_ref[s * cap:(s + 1) * cap, :] = jnp.where(filled, code, 0.0).astype(jnp.bfloat16)


def finish(z, off, filled, inverse):
    slots = z.shape[0] // 2
    width = inverse.shape[0]
    senders = 4
    step = senders * (slots // filled.shape[0])
    return pl.pallas_call(
        functools.partial(finish_kernel, senders),
        out_shape=jax.ShapeDtypeStruct((slots, width), jnp.bfloat16),
        grid=(slots // step,),
        in_specs=[
            pl.BlockSpec((2 * step, 128), lambda s: (s, 0)),
            pl.BlockSpec((2 * step, 128), lambda s: (s, 0)),
            smem(),
            pl.BlockSpec((width, 2 * width), lambda s: (0, 0)),
        ],
        out_specs=pl.BlockSpec((step, width), lambda s: (s, 0)),
        compiler_params=limits(),
        cost_estimate=pl.CostEstimate(flops=2 * 10**9, bytes_accessed=13 * 10**6, transcendentals=0),
        name="finish",
    )(z, off, filled, inverse)


exact_mode = lax.Precision.HIGHEST
PIVOT_LEAST = 1.0 / 64.0


def orthonormal(product):
    gram_matrix = jnp.dot(product.T, product, precision=exact_mode, preferred_element_type=jnp.float32)
    lower = jnp.linalg.cholesky(gram_matrix)
    return jax.scipy.linalg.solve_triangular(lower, product.T, lower=True).T


def careful(tri, start, x, centroids, pos, ids):
    owners = lax.axis_size("dev")
    slots = ids.shape[0]
    grid = [[None] * 8 for _ in range(8)]
    for i in range(8):
        for j in range(i + 1):
            at = STARTS[(i, j)]
            grid[i][j] = tri[at:at + 128]
            grid[j][i] = tri[at:at + 128].T
    moment = jnp.block(grid)
    basis = start
    for sweep in range(2):
        product = jnp.dot(moment, basis, precision=exact_mode, preferred_element_type=jnp.float32)
        basis = orthonormal(product)
    width = start.shape[1]
    pos = pos.reshape(-1)
    pos = pos // (2 * CAP) * CAP + pos % (2 * CAP)
    projected = jnp.dot(x, basis, precision=exact_mode, preferred_element_type=jnp.float32)
    sent = jnp.zeros((slots, width), jnp.float32).at[pos].set(projected)
    sent = sent.reshape(owners, slots // owners, width)
    values = lax.all_to_all(sent, "dev", split_axis=0, concat_axis=0, tiled=True).reshape(slots, width)
    offsets = jnp.dot(centroids, basis, precision=exact_mode, preferred_element_type=jnp.float32)
    code = values - jnp.take(offsets, jnp.maximum(ids, 0), axis=0)
    return jnp.where(ids[:, None] >= 0, code, 0.0).astype(jnp.bfloat16)


def shards(corpus_rows, list_ids, source_ids, list_slot, centroids, start_basis):
    owners = lax.axis_size("dev")
    lists_dev = centroids.shape[0]
    slots = owners * CAP
    tri, pos, arrived, counts = front(corpus_rows, list_ids, source_ids, list_slot, owners, lists_dev, CAP)
    sent, basis, gram = project(tri, start_basis, corpus_rows, pos, owners, CAP)
    values = lax.all_to_all(
        sent.reshape(owners, 2 * CAP, 128), "dev", split_axis=0, concat_axis=0, tiled=True
    ).reshape(2 * slots, 128)
    ids = arrived[:, :2].reshape(owners, 256)[:, :CAP]
    filled = jnp.sum((ids >= 0).astype(jnp.int32), axis=1)
    ids = ids.reshape(slots)
    row_sources = arrived[:, 2:].reshape(owners, 256)[:, :CAP].reshape(slots)
    inverse, pivots = factor(gram)
    off = offsets_at(centroids, basis, ids, CAP)
    row_codes = lax.cond(
        jnp.min(pivots) >= PIVOT_LEAST,
        lambda: finish(values, off, filled, inverse),
        lambda: careful(tri, start_basis, corpus_rows, centroids, pos, ids),
    )
    return row_codes, row_sources, counts.reshape(lists_dev)


def solution(mesh):
    placed = (
        P(("group", "dev"), None),
        P(("group", "dev")),
        P(("group", "dev")),
        P(),
        P("dev", None),
        P(),
    )
    return jax.shard_map(
        shards,
        mesh=mesh,
        in_specs=placed,
        out_specs=(P(("group", "dev"), None), P(("group", "dev")), P("dev")),
        check_vma=False,
    )
```

```python
import functools
import jax
import jax.numpy as jnp
from jax import lax
from jax.experimental import pallas as pl
from jax.experimental.pallas import tpu as pltpu
from jax.sharding import PartitionSpec as P

CAP = 160
MESH = pl.DeviceIdType.MESH
NT = (((1,), (1,)), ((), ()))
TN = (((0,), (0,)), ((), ()))
HALF, MID, LOW = 1152, 288, 72
PAIRS = ((0, 0), (1, 0), (1, 1), (2, 0), (2, 1), (2, 2), (3, 0), (3, 1), (3, 2), (3, 3))


def block_starts():
    starts = {}
    for i, j in PAIRS:
        for a in range(2):
            for b in range(2):
                if 2 * j + b <= 2 * i + a:
                    starts[(2 * i + a, 2 * j + b)] = len(starts) * 128
    return starts


STARTS = block_starts()


def vmem():
    return pl.BlockSpec(memory_space=pltpu.VMEM)


def smem():
    return pl.BlockSpec(memory_space=pltpu.SMEM)


def limits():
    return pltpu.CompilerParams(vmem_limit_bytes=48 * 2**20)


def halves(v):
    top = v.astype(jnp.bfloat16)
    return top, (v - top.astype(jnp.float32)).astype(jnp.bfloat16)


def dot(a, b, dims=(((1,), (0,)), ((), ()))):
    return lax.dot_general(a, b, dims, preferred_element_type=jnp.float32)


def packed_rows(cap):
    return cap + cap // 2 + 8


def narrow(flag):
    return flag.astype(jnp.float32).astype(jnp.bfloat16)


def place_rows(ids, source, table, owners, lists_dev, cap):
    count = ids.shape[1]
    sub = lax.broadcasted_iota(jnp.int32, (table.shape[0], count), 0)
    row_hit = narrow(sub == ids // 128)
    high = dot((table // 256).astype(jnp.float32).astype(jnp.bfloat16), row_hit, TN)
    low = dot((table % 256).astype(jnp.float32).astype(jnp.bfloat16), row_hit, TN)
    lane = lax.broadcasted_iota(jnp.int32, (128, count), 0)
    slot = jnp.sum(jnp.where(lane == ids % 128, high * 256.0 + low, 0.0), axis=0, keepdims=True).astype(jnp.int32)
    owner = slot // lists_dev
    local = slot % lists_dev
    owner_one = narrow(lax.broadcasted_iota(jnp.int32, (owners, count), 0) == owner)
    width = 256
    square = (width, width)
    before = narrow(lax.broadcasted_iota(jnp.int32, square, 0) < lax.broadcasted_iota(jnp.int32, square, 1))
    seen = jnp.zeros((owners, 1), jnp.float32)
    ranks = []
    for k in range(count // width):
        part = owner_one[:, k * width:(k + 1) * width]
        prior = dot(part, before) + seen
        part = part.astype(jnp.float32)
        ranks.append(jnp.sum(prior * part, axis=0, keepdims=True))
        seen = seen + jnp.sum(part, axis=1, keepdims=True)
    rank = jnp.concatenate(ranks, axis=1).astype(jnp.int32)
    rank_hit = lax.broadcasted_iota(jnp.int32, (256, count), 0) == rank

    def collect(value):
        picked = jnp.where(rank_hit, value.astype(jnp.float32), 0.0).astype(jnp.bfloat16)
        return dot(owner_one, picked, NT)

    filled = collect(jnp.ones((1, count), jnp.int32)) > 0.5
    local_at = collect(local // 256) * 256.0 + collect(local % 256)
    source_at = collect(source // 16384) * 16384.0 + collect((source // 128) % 128) * 128.0 + collect(source % 128)
    ids_at = jnp.where(filled, local_at, -1.0).astype(jnp.int32)
    sources_at = jnp.where(filled, source_at, -1.0).astype(jnp.int32)
    pos = jnp.concatenate([owner * cap + rank, owner * packed_rows(cap) + rank], axis=0)
    return pos, ids_at, sources_at


def front_kernel(lists_dev, cap, x_hbm, list_hbm, source_hbm, table_hbm, tri_ref, pos_ref, got_ref, count_ref,
                 x_ref, list_ref, source_ref, table_ref, load_s, dest, part, core_buf, first_buf, sum_buf, second_buf, mid_sum, tile_buf, tally, tally_buf,
                 core_s, core_r, first_s, first_r, second_s, second_r, tile_s, tile_r, top_s, top_r, odd_s, odd_r,
                 fan_s, fan_r, row_s, row_r, pair_s, pair_r, wide_s, wide_r, id_s, id_r, tally_s, tally_r):
    z = lax.axis_index("group")
    dev = lax.axis_index("dev")
    owners = 32
    x, y, c = dev // 8, (dev // 2) % 4, dev % 2

    def at(xx, yy):
        return (z, (xx * 4 + yy) * 2 + c)

    other = (z, dev + 1 - 2 * c)
    along_x = [at((x + d) % 4, y) for d in (1, 2, 3)]
    along_y = [at(x, (y + d) % 4) for d in (1, 2, 3)]
    along_z = [((z + d) % 8, dev) for d in range(1, 8)]
    barrier = pltpu.get_barrier_semaphore()
    for k in range(1, owners):
        pl.semaphore_signal(barrier, inc=1, device_id=(z, (dev + k) % owners), device_id_type=MESH)
    for peer in along_z:
        pl.semaphore_signal(barrier, inc=1, device_id=peer, device_id_type=MESH)

    loads = [
        pltpu.make_async_copy(list_hbm, list_ref, load_s.at[4]),
        pltpu.make_async_copy(source_hbm, source_ref, load_s.at[5]),
        pltpu.make_async_copy(table_hbm, table_ref, load_s.at[6]),
    ]
    for k in range(4):
        columns = pl.ds(k * 256, 256)
        loads.append(pltpu.make_async_copy(x_hbm.at[:, columns], x_ref.at[:, columns], load_s.at[k]))
    for load in loads[3:] + loads[:3]:
        load.start()
    sent = []

    def copy_to(src, dst, s, r, peer):
        return pltpu.make_async_remote_copy(src_ref=src, dst_ref=dst, send_sem=s, recv_sem=r, device_id=peer,
                                            device_id_type=MESH)

    def send(src, dst, s, r, peer):
        copy = copy_to(src, dst, s, r, peer)
        copy.start()
        sent.append(copy)
        return copy

    def span(start, size):
        return pl.ds(pl.multiple_of(start, 8), size)

    lefts = {}

    def moment(pairs):
        for i, j in pairs:
            if i not in lefts:
                loads[3 + i].wait()
                lefts[i] = x_ref[:, i * 256:(i + 1) * 256].T
            square = dot(lefts[i], x_ref[:, j * 256:(j + 1) * 256])
            for a in range(2):
                for b in range(2):
                    key = (2 * i + a, 2 * j + b)
                    if key in STARTS:
                        begin = STARTS[key]
                        part[begin:begin + 128, :] = square[a * 128:(a + 1) * 128, b * 128:(b + 1) * 128]

    base = [p * 2 * HALF + c * HALF for p in range(2)]
    firsts = [(x, along_x), (y, along_y)]
    seconds = [(y, along_y), (x, along_x)]
    core = [None, None]
    first = [{}, {}]

    def swap(p):
        core[p] = send(part.at[span(p * 2 * HALF + (1 - c) * HALF, HALF)], core_buf.at[p], core_s.at[p], core_r.at[p],
                       other)

    def down_first(p):
        core[p].wait_recv()
        core_buf[p] = core_buf[p] + part[span(base[p], HALF), :]
        f, peers = firsts[p]
        s = seconds[p][0]
        for k in range(4):
            for d in (1, 2, 3):
                begin = ((f + d) % 4) * MID + ((s + 1 + k) % 4) * LOW
                first[p][k, d] = send(core_buf.at[p, span(begin, LOW)], first_buf.at[p, d - 1, k],
                                      first_s.at[p, d - 1, k], first_r.at[p, d - 1, k], peers[d - 1])

    moment(PAIRS[:5])
    pl.semaphore_wait(barrier, 38)
    swap(0)
    moment(PAIRS[5:])
    swap(1)
    down_first(0)
    down_first(1)
    for load in loads[:3]:
        load.wait()
    pos, ids_at, sources_at = place_rows(list_ref[...], source_ref[...], table_ref[...], owners, lists_dev, cap)
    pos_ref[...] = pos
    dest[:, 0, :] = ids_at[:, :128]
    dest[:, 1, :] = ids_at[:, 128:]
    dest[:, 2, :] = sources_at[:, :128]
    dest[:, 3, :] = sources_at[:, 128:]
    second = [{}, {}]
    for k in range(4):
        for p in range(2):
            f = firsts[p][0]
            s, peers = seconds[p]
            for d in (1, 2, 3):
                first[p][k, d].wait_recv()
            own = core_buf[p, span(f * MID + ((s + 1 + k) % 4) * LOW, LOW), :]
            sum_buf[p, k] = (own + first_buf[p, 0, k]) + (first_buf[p, 1, k] + first_buf[p, 2, k])
            if k < 3:
                second[p][k] = send(sum_buf.at[p, k], second_buf.at[p, k], second_s.at[p, k], second_r.at[p, k], peers[k])
    tile = [[], []]
    for p in range(2):
        for k in range(3):
            second[p][k].wait_recv()
        mid_sum[p] = (sum_buf[p, 3] + second_buf[p, 0]) + (second_buf[p, 1] + second_buf[p, 2])
        for d in range(1, 8):
            tile[p].append(send(mid_sum.at[p, span(((z + d) % 8) * 8, 16)], tile_buf.at[p, d - 1],
                                tile_s.at[p, d - 1], tile_r.at[p, d - 1], along_z[d - 1]))
    arrive = []
    for k in range(1, owners):
        peer = (dev + k) % owners
        arrive.append(send(dest.at[peer], got_ref.at[dev], id_s.at[k - 1], id_r.at[k - 1], (z, peer)))
    got_ref[dev] = dest[dev]
    def hand(begin, size, s, r, peer):
        return send(tri_ref.at[span(begin, size)], tri_ref.at[span(begin, size)], s, r, peer)

    top = [[], []]

    def odd(p, d):
        begin = base[p] + firsts[p][0] * MID + seconds[p][0] * LOW + 64
        return copy_to(tri_ref.at[span(begin, 8)], tri_ref.at[span(begin, 8)], odd_s.at[p, d - 1], odd_r.at[p],
                       along_z[d - 1])

    for p in range(2):
        for copy in tile[p]:
            copy.wait_recv()
        total = mid_sum[p, span(z * 8, 16), :]
        for d in range(7):
            total = total + tile_buf[p, d]
        begin = base[p] + firsts[p][0] * MID + seconds[p][0] * LOW
        tri_ref[span(begin + z * 8, 8), :] = total[:8]
        for d in range(1, 8):
            top[p].append(hand(begin + z * 8, 8, top_s.at[p, d - 1], top_r.at[p, d - 1], along_z[d - 1]))

        @pl.when(z == 7)
        def _():
            tri_ref[span(begin + 64, 8), :] = total[8:]
            for d in range(1, 8):
                odd(p, d).start()

    for copy in arrive:
        copy.wait_recv()
    ids = jnp.concatenate([got_ref[:, 0, :], got_ref[:, 1, :]], axis=0)
    ids = jnp.concatenate([ids[k:k + 1, :] for k in range(2 * owners)], axis=1)
    count = ids.shape[1]
    high = lax.broadcasted_iota(jnp.int32, (16, count), 0) == jnp.where(ids >= 0, ids // 128, -1)
    low = lax.broadcasted_iota(jnp.int32, (128, count), 0) == ids % 128
    tally[...] = dot(narrow(high), narrow(low), NT)
    tallies = [send(tally, tally_buf.at[d - 1], tally_s.at[d - 1], tally_r.at[d - 1], along_z[d - 1])
               for d in range(1, 8)]

    fan = [{}, {}]
    row = [{}, {}]
    pair = [[], []]

    def outward(p, k):
        f, peers = firsts[p]
        begin = base[p] + f * MID + ((seconds[p][0] - k + 4) % 4) * LOW
        for d in (1, 2, 3):
            row[p][k, d] = hand(begin, LOW, row_s.at[p, k, d - 1], row_r.at[p, k, d - 1], peers[d - 1])
        pair[p].append(hand(begin, LOW, pair_s.at[p, k], pair_r.at[p, k], other))

    for p in range(2):
        for copy in top[p]:
            copy.wait_recv()

        @pl.when(z != 7)
        def _():
            odd(p, 1).wait_recv()

        s, peers = seconds[p]
        begin = base[p] + firsts[p][0] * MID + s * LOW
        for d in (1, 2, 3):
            fan[p][d] = hand(begin, LOW, fan_s.at[p, d - 1], fan_r.at[p, d - 1], peers[d - 1])
        outward(p, 0)
    for d in (1, 2, 3):
        for p in range(2):
            fan[p][d].wait_recv()
            outward(p, d)
    total = tally[...]
    for d in range(7):
        tallies[d].wait_recv()
        total = total + tally_buf[d]
    count_ref[...] = total.astype(jnp.int32)
    wide = [[], []]
    for d in (1, 2, 3):
        for p in range(2):
            for k in range(4):
                row[p][k, d].wait_recv()
            begin = base[p] + ((firsts[p][0] - d + 4) % 4) * MID
            wide[p].append(hand(begin, MID, wide_s.at[p, d - 1], wide_r.at[p, d - 1], other))
    for p in range(2):
        for copy in pair[p] + wide[p]:
            copy.wait_recv()
    for copy in sent:
        copy.wait_send()

    @pl.when(z == 7)
    def _():
        for p in range(2):
            for d in range(1, 8):
                odd(p, d).wait_send()


def front(corpus_rows, list_ids, source_ids, list_slot, owners, lists_dev, cap):
    count = list_ids.shape[0]
    sem = pltpu.SemaphoreType.DMA
    f32 = jnp.float32
    return pl.pallas_call(
        functools.partial(front_kernel, lists_dev, cap),
        out_shape=(
            jax.ShapeDtypeStruct((4 * HALF, 128), f32),
            jax.ShapeDtypeStruct((2, count), jnp.int32),
            jax.ShapeDtypeStruct((owners, 4, 128), jnp.int32),
            jax.ShapeDtypeStruct((lists_dev // 128, 128), jnp.int32),
        ),
        in_specs=[pl.BlockSpec(memory_space=pl.ANY)] * 4,
        out_specs=(vmem(),) * 4,
        scratch_shapes=[
            pltpu.VMEM(corpus_rows.shape, jnp.bfloat16),
            pltpu.VMEM((1, count), jnp.int32),
            pltpu.VMEM((1, count), jnp.int32),
            pltpu.VMEM((list_slot.shape[0] // 128, 128), jnp.int32),
            sem((7,)),
            pltpu.VMEM((owners, 4, 128), jnp.int32),
            pltpu.VMEM((4 * HALF, 128), f32),
            pltpu.VMEM((2, HALF, 128), f32),
            pltpu.VMEM((2, 3, 4, LOW, 128), f32),
            pltpu.VMEM((2, 4, LOW, 128), f32),
            pltpu.VMEM((2, 3, LOW, 128), f32),
            pltpu.VMEM((2, LOW, 128), f32),
            pltpu.VMEM((2, 7, 16, 128), f32),
            pltpu.VMEM((16, 128), f32),
            pltpu.VMEM((7, 16, 128), f32),
            sem((2,)), sem((2,)), sem((2, 3, 4)), sem((2, 3, 4)), sem((2, 3)), sem((2, 3)), sem((2, 7)), sem((2, 7)),
            sem((2, 7)), sem((2, 7)), sem((2, 7)), sem((2,)), sem((2, 3)), sem((2, 3)), sem((2, 4, 3)), sem((2, 4, 3)),
            sem((2, 4)), sem((2, 4)), sem((2, 3)), sem((2, 3)), sem((31,)), sem((31,)), sem((7,)), sem((7,)),
        ],
        compiler_params=pltpu.CompilerParams(collective_id=0, has_side_effects=True, vmem_limit_bytes=60 * 2**20),
        cost_estimate=pl.CostEstimate(flops=10**10, bytes_accessed=10**8, transcendentals=0),
        name="front",
    )(corpus_rows, list_ids.reshape(1, count), source_ids.reshape(1, count), list_slot.reshape(-1, 128))


def step_of(exponent):
    return jnp.exp2((exponent - 23).astype(jnp.float32))


def project_rows(rows_ref, basis_ref, z_ref):
    count = rows_ref.shape[0]
    width = basis_ref.shape[1] // 2
    step = 1024
    for begin in range(0, count, step):
        both = dot(rows_ref[begin:begin + step, :], basis_ref[...])
        code = both[:, :width] + both[:, width:]
        z_ref[begin:begin + step, :] = code[:, :128]
        z_ref[count + begin:count + begin + step, :] = code[:, 128:]


def project_kernel(cap, tri_ref, start_ref, x_hbm, pos_ref, out_ref, basis_ref, gram_ref, x_ref, load_s, m_hi, m_lo,
                   z_ref, word_ref, tail_ref, sent_ref):
    load = pltpu.make_async_copy(x_hbm, x_ref, load_s)
    load.start()
    eye = lax.broadcasted_iota(jnp.int32, (128, 128), 0) == lax.broadcasted_iota(jnp.int32, (128, 128), 1)
    peak = jnp.zeros((128, 128), jnp.float32)
    for i in range(8):
        for j in range(i + 1):
            at = STARTS[(i, j)]
            block = tri_ref[at:at + 128, :]
            hi, lo = halves(block)
            m_hi[i * 128:(i + 1) * 128, j * 128:(j + 1) * 128] = hi
            m_lo[i * 128:(i + 1) * 128, j * 128:(j + 1) * 128] = lo
            if i != j:
                hi, lo = halves(block.T)
                m_hi[j * 128:(j + 1) * 128, i * 128:(i + 1) * 128] = hi
                m_lo[j * 128:(j + 1) * 128, i * 128:(i + 1) * 128] = lo
            else:
                peak = jnp.maximum(peak, jnp.where(eye, block, 0.0))
    scale = 1.0 / jnp.max(jnp.max(peak, axis=0, keepdims=True), axis=1, keepdims=True)
    width = start_ref.shape[1]

    def times_moment(v):
        hi, lo = halves(v * scale)
        both = dot(m_hi[...], jnp.concatenate([hi, lo], axis=1))
        return (both[:, :width] + both[:, width:]) + dot(m_lo[...], hi)

    product = times_moment(times_moment(start_ref[...]))
    product = product * lax.rsqrt(jnp.sum(product * product, axis=0, keepdims=True))
    hi, lo = halves(product)
    basis_ref[:, :width] = hi
    basis_ref[:, width:] = lo
    cross = dot(hi, basis_ref[...], TN)
    mixed = cross[:, width:]
    gram_ref[...] = cross[:, :width] + (mixed + mixed.T)
    load.wait()
    project_rows(x_ref, basis_ref, z_ref)
    count = x_ref.shape[0]

    peak = jnp.max(jnp.max(jnp.abs(z_ref[...]), axis=0, keepdims=True), axis=1, keepdims=True)
    lane = lax.broadcasted_iota(jnp.int32, (1, 128), 1)
    below = jnp.where(peak >= jnp.exp2((lane - 64).astype(jnp.float32)), 1.0, 0.0)
    exponent = jnp.sum(below, axis=1, keepdims=True).astype(jnp.int32) - 64
    unit = 1.0 / step_of(exponent)
    most = float(2**23 - 1)
    step = 256

    @pl.loop(0, count // step)
    def _(k):
        at = pl.multiple_of(k * step, step)

        def coded(begin):
            return jnp.clip(jnp.round(z_ref[pl.ds(begin, step), :] * unit), -most, most).astype(jnp.int32)

        low = coded(at)
        high = coded(pl.multiple_of(at + count, step))
        word_ref[pl.ds(at, step), :] = (low << 8) | (high & 255)
        upper = high >> 8
        tail_ref[pl.ds(at, step), :] = (upper << 16) | (pltpu.roll(upper, 64, 1) & 65535)

    @pl.loop(0, count // 16)
    def _(k):
        for u in range(16):
            row = k * 16 + u
            out_ref[pl.ds(pos_ref[1, row], 1), :] = word_ref[pl.ds(row, 1), :]
            sent_ref[pl.ds(pos_ref[0, row], 1), :] = tail_ref[pl.ds(row, 1), :]

    half = cap // 2
    left = lax.broadcasted_iota(jnp.int32, (half, 128), 1) < 64
    for owner in range(sent_ref.shape[0] // cap):
        begin = owner * packed_rows(cap) + cap
        first = sent_ref[owner * cap:owner * cap + half, :]
        second = sent_ref[owner * cap + half:(owner + 1) * cap, :]
        out_ref[begin:begin + half, :] = jnp.where(left, first, pltpu.roll(second, 64, 1))
        out_ref[begin + half:begin + half + 8, :] = jnp.broadcast_to(exponent, (8, 128))


def project(tri, start, x, pos, owners, cap):
    feature, width = start.shape
    return pl.pallas_call(
        functools.partial(project_kernel, cap),
        out_shape=(
            jax.ShapeDtypeStruct((owners * packed_rows(cap), 128), jnp.int32),
            jax.ShapeDtypeStruct((feature, 2 * width), jnp.bfloat16),
            jax.ShapeDtypeStruct((width, width), jnp.float32),
        ),
        in_specs=[vmem(), vmem(), pl.BlockSpec(memory_space=pl.ANY), smem()],
        out_specs=(vmem(), vmem(), vmem()),
        scratch_shapes=[
            pltpu.VMEM(x.shape, jnp.bfloat16),
            pltpu.SemaphoreType.DMA,
            pltpu.VMEM((feature, feature), jnp.bfloat16),
            pltpu.VMEM((feature, feature), jnp.bfloat16),
            pltpu.VMEM((2 * x.shape[0], 128), jnp.float32),
            pltpu.VMEM((x.shape[0], 128), jnp.int32),
            pltpu.VMEM((x.shape[0], 128), jnp.int32),
            pltpu.VMEM((owners * cap, 128), jnp.int32),
        ],
        compiler_params=limits(),
        cost_estimate=pl.CostEstimate(flops=10**10, bytes_accessed=2 * 10**7, transcendentals=0),
        name="project",
    )(tri, start, x, pos)


def factor_kernel(gram_ref, inverse_ref, pivot_ref, aug):
    size = gram_ref.shape[0]
    block = 32
    panel = 8
    aug[:, :size] = gram_ref[...]
    aug[:, size:] = (
        lax.broadcasted_iota(jnp.int32, (size, size), 0) == lax.broadcasted_iota(jnp.int32, (size, size), 1)
    ).astype(jnp.float32)
    row_at = lax.broadcasted_iota(jnp.int32, (block, 128), 0)
    lane_at = lax.broadcasted_iota(jnp.int32, (block, 128), 1)
    least = jnp.full((1, 128), 1e30, jnp.float32)
    for b in range(size // block):
        lo, hi = b * block, (b + 1) * block
        square = aug[lo:hi, lo:hi]
        unit = (row_at[:, :block] == lane_at[:, :block]).astype(jnp.float32)
        work = jnp.concatenate([square, unit, jnp.zeros((block, 128 - 2 * block), jnp.float32)], axis=1)
        for p in range(block // panel):
            cols = [
                jnp.broadcast_to(work[:, p * panel + j:p * panel + j + 1], (block, 128)) for j in range(panel)
            ]
            for j in range(panel):
                k = p * panel + j
                pivot = cols[j][k:k + 1, :]
                least = jnp.minimum(least, pivot)
                root = lax.rsqrt(pivot)
                column = jnp.where(row_at > k, cols[j] * root, 0.0)
                for jj in range(j + 1, panel):
                    kk = p * panel + jj
                    cols[jj] = cols[jj] - column * column[kk:kk + 1, :]
                row = work[k:k + 1, :] * root
                work = jnp.where(row_at == k, row, work - column * row)
        inverse = work[:, block:2 * block]
        rows = lax.dot_general(inverse, aug[lo:hi, :], (((1,), (0,)), ((), ())), precision=lax.Precision.HIGHEST,
                               preferred_element_type=jnp.float32)
        aug[lo:hi, :] = rows
        if hi < size:
            below = rows[:, hi:size].T
            aug[hi:, :] -= lax.dot_general(below, rows, (((1,), (0,)), ((), ())), precision=lax.Precision.HIGHEST,
                                           preferred_element_type=jnp.float32)
    whole = aug[:, size:].T
    top, bottom = halves(whole)
    inverse_ref[:, :size] = top
    inverse_ref[:, size:] = bottom
    pivot_ref[...] = least


def factor(gram):
    size = gram.shape[0]
    return pl.pallas_call(
        factor_kernel,
        out_shape=(
            jax.ShapeDtypeStruct((size, 2 * size), jnp.bfloat16),
            jax.ShapeDtypeStruct((1, 128), jnp.float32),
        ),
        in_specs=[vmem()],
        out_specs=(vmem(), vmem()),
        scratch_shapes=[pltpu.VMEM((size, 2 * size), jnp.float32)],
        compiler_params=limits(),
        cost_estimate=pl.CostEstimate(flops=10**9, bytes_accessed=10**7, transcendentals=0),
        name="factor",
    )(gram)


def offset_kernel(cap, c_ref, basis_ref, id_ref, out_ref, z_ref):
    project_rows(c_ref, basis_ref, z_ref)
    count = c_ref.shape[0]

    @pl.loop(0, id_ref.shape[0] // cap)
    def _(sender):
        @pl.loop(0, cap // 16)
        def _(k):
            for u in range(16):
                rank = k * 16 + u
                row = jnp.maximum(id_ref[sender * cap + rank], 0)
                slot = sender * (2 * cap) + rank
                out_ref[pl.ds(slot, 1), :] = z_ref[pl.ds(row, 1), :]
                out_ref[pl.ds(slot + cap, 1), :] = z_ref[pl.ds(row + count, 1), :]


def offsets_at(centroids, basis, ids, cap):
    return pl.pallas_call(
        functools.partial(offset_kernel, cap),
        out_shape=jax.ShapeDtypeStruct((2 * ids.shape[0], 128), jnp.float32),
        in_specs=[vmem(), vmem(), smem()],
        out_specs=vmem(),
        scratch_shapes=[pltpu.VMEM((2 * centroids.shape[0], 128), jnp.float32)],
        compiler_params=limits(),
        cost_estimate=pl.CostEstimate(flops=10**10, bytes_accessed=10**7, transcendentals=0),
        name="offsets",
    )(centroids, basis, ids)


def finish_kernel(senders, z_ref, off_ref, count_ref, inverse_ref, out_ref):
    width = out_ref.shape[1]
    cap = out_ref.shape[0] // senders
    rank = lax.broadcasted_iota(jnp.int32, (cap, width), 0)
    half = cap // 2
    left = lax.broadcasted_iota(jnp.int32, (half, 128), 1) < 64
    for s in range(senders):
        begin = s * packed_rows(cap)
        word = z_ref[begin:begin + cap, :]
        tail = z_ref[begin + cap:begin + cap + half, :]
        unit = step_of(z_ref[begin + cap + half:begin + cap + half + 1, :])
        upper = tail >> 16
        under = (tail << 16) >> 16
        first = jnp.where(left, upper, pltpu.roll(under, 64, 1))
        second = jnp.where(left, pltpu.roll(upper, 64, 1), under)
        high = (jnp.concatenate([first, second], axis=0) << 8) | (word & 255)
        begin = 2 * s * cap
        low = (word >> 8).astype(jnp.float32) * unit - off_ref[begin:begin + cap, :]
        high = high.astype(jnp.float32) * unit - off_ref[begin + cap:begin + 2 * cap, :]
        hi, lo = halves(jnp.concatenate([low, high], axis=1))
        both = dot(hi, inverse_ref[...])
        code = (both[:, :width] + both[:, width:]) + dot(lo, inverse_ref[:, :width])
        filled = rank < count_ref[pl.program_id(0) * senders + s]
        out_ref[s * cap:(s + 1) * cap, :] = jnp.where(filled, code, 0.0).astype(jnp.bfloat16)


def finish(z, off, filled, inverse):
    owners = filled.shape[0]
    slots = off.shape[0] // 2
    width = inverse.shape[0]
    senders = 4
    step = senders * (slots // owners)
    return pl.pallas_call(
        functools.partial(finish_kernel, senders),
        out_shape=jax.ShapeDtypeStruct((slots, width), jnp.bfloat16),
        grid=(slots // step,),
        in_specs=[
            pl.BlockSpec((z.shape[0] // owners * senders, 128), lambda s: (s, 0)),
            pl.BlockSpec((2 * step, 128), lambda s: (s, 0)),
            smem(),
            pl.BlockSpec((width, 2 * width), lambda s: (0, 0)),
        ],
        out_specs=pl.BlockSpec((step, width), lambda s: (s, 0)),
        compiler_params=limits(),
        cost_estimate=pl.CostEstimate(flops=2 * 10**9, bytes_accessed=13 * 10**6, transcendentals=0),
        name="finish",
    )(z, off, filled, inverse)


exact_mode = lax.Precision.HIGHEST
PIVOT_LEAST = 1.0 / 64.0


def orthonormal(product):
    gram_matrix = jnp.dot(product.T, product, precision=exact_mode, preferred_element_type=jnp.float32)
    lower = jnp.linalg.cholesky(gram_matrix)
    return jax.scipy.linalg.solve_triangular(lower, product.T, lower=True).T


def careful(tri, start, x, centroids, pos, ids):
    owners = lax.axis_size("dev")
    slots = ids.shape[0]
    grid = [[None] * 8 for _ in range(8)]
    for i in range(8):
        for j in range(i + 1):
            at = STARTS[(i, j)]
            grid[i][j] = tri[at:at + 128]
            grid[j][i] = tri[at:at + 128].T
    moment = jnp.block(grid)
    basis = start
    for sweep in range(2):
        product = jnp.dot(moment, basis, precision=exact_mode, preferred_element_type=jnp.float32)
        basis = orthonormal(product)
    width = start.shape[1]
    projected = jnp.dot(x, basis, precision=exact_mode, preferred_element_type=jnp.float32)
    sent = jnp.zeros((slots, width), jnp.float32).at[pos[0]].set(projected)
    sent = sent.reshape(owners, slots // owners, width)
    values = lax.all_to_all(sent, "dev", split_axis=0, concat_axis=0, tiled=True).reshape(slots, width)
    offsets = jnp.dot(centroids, basis, precision=exact_mode, preferred_element_type=jnp.float32)
    code = values - jnp.take(offsets, jnp.maximum(ids, 0), axis=0)
    return jnp.where(ids[:, None] >= 0, code, 0.0).astype(jnp.bfloat16)


def shards(corpus_rows, list_ids, source_ids, list_slot, centroids, start_basis):
    owners = lax.axis_size("dev")
    lists_dev = centroids.shape[0]
    slots = owners * CAP
    tri, pos, arrived, counts = front(corpus_rows, list_ids, source_ids, list_slot, owners, lists_dev, CAP)
    sent, basis, gram = project(tri, start_basis, corpus_rows, pos, owners, CAP)
    values = lax.all_to_all(
        sent.reshape(owners, packed_rows(CAP), 128), "dev", split_axis=0, concat_axis=0, tiled=True
    ).reshape(owners * packed_rows(CAP), 128)
    ids = arrived[:, :2].reshape(owners, 256)[:, :CAP]
    filled = jnp.sum((ids >= 0).astype(jnp.int32), axis=1)
    ids = ids.reshape(slots)
    row_sources = arrived[:, 2:].reshape(owners, 256)[:, :CAP].reshape(slots)
    inverse, pivots = factor(gram)
    off = offsets_at(centroids, basis, ids, CAP)
    row_codes = lax.cond(
        jnp.min(pivots) >= PIVOT_LEAST,
        lambda: finish(values, off, filled, inverse),
        lambda: careful(tri, start_basis, corpus_rows, centroids, pos, ids),
    )
    return row_codes, row_sources, counts.reshape(lists_dev)


def solution(mesh):
    placed = (
        P(("group", "dev"), None),
        P(("group", "dev")),
        P(("group", "dev")),
        P(),
        P("dev", None),
        P(),
    )
    return jax.shard_map(
        shards,
        mesh=mesh,
        in_specs=placed,
        out_specs=(P(("group", "dev"), None), P(("group", "dev")), P("dev")),
        check_vma=False,
    )
```

```python
import functools
import jax
import jax.numpy as jnp
from jax import lax
from jax.experimental import pallas as pl
from jax.experimental.pallas import tpu as pltpu
from jax.sharding import PartitionSpec as P

CAP = 160
MESH = pl.DeviceIdType.MESH
NT = (((1,), (1,)), ((), ()))
TN = (((0,), (0,)), ((), ()))
HALF, MID, LOW = 1152, 288, 72
PAIRS = ((0, 0), (1, 0), (1, 1), (2, 0), (2, 1), (2, 2), (3, 0), (3, 1), (3, 2), (3, 3))


def block_starts():
    starts = {}
    for i, j in PAIRS:
        for a in range(2):
            for b in range(2):
                if 2 * j + b <= 2 * i + a:
                    starts[(2 * i + a, 2 * j + b)] = len(starts) * 128
    return starts


STARTS = block_starts()


def vmem():
    return pl.BlockSpec(memory_space=pltpu.VMEM)


def smem():
    return pl.BlockSpec(memory_space=pltpu.SMEM)


def limits():
    return pltpu.CompilerParams(vmem_limit_bytes=48 * 2**20)


def halves(v):
    top = v.astype(jnp.bfloat16)
    return top, (v - top.astype(jnp.float32)).astype(jnp.bfloat16)


def dot(a, b, dims=(((1,), (0,)), ((), ()))):
    return lax.dot_general(a, b, dims, preferred_element_type=jnp.float32)


def packed_rows(cap):
    return cap + cap // 2 + 8


def narrow(flag):
    return flag.astype(jnp.float32).astype(jnp.bfloat16)


def place_rows(ids, source, table, owners, lists_dev, cap):
    count = ids.shape[1]
    sub = lax.broadcasted_iota(jnp.int32, (table.shape[0], count), 0)
    row_hit = narrow(sub == ids // 128)
    high = dot((table // 256).astype(jnp.float32).astype(jnp.bfloat16), row_hit, TN)
    low = dot((table % 256).astype(jnp.float32).astype(jnp.bfloat16), row_hit, TN)
    lane = lax.broadcasted_iota(jnp.int32, (128, count), 0)
    slot = jnp.sum(jnp.where(lane == ids % 128, high * 256.0 + low, 0.0), axis=0, keepdims=True).astype(jnp.int32)
    owner = slot // lists_dev
    local = slot % lists_dev
    owner_one = narrow(lax.broadcasted_iota(jnp.int32, (owners, count), 0) == owner)
    width = 256
    square = (width, width)
    before = narrow(lax.broadcasted_iota(jnp.int32, square, 0) < lax.broadcasted_iota(jnp.int32, square, 1))
    seen = jnp.zeros((owners, 1), jnp.float32)
    ranks = []
    for k in range(count // width):
        part = owner_one[:, k * width:(k + 1) * width]
        prior = dot(part, before) + seen
        part = part.astype(jnp.float32)
        ranks.append(jnp.sum(prior * part, axis=0, keepdims=True))
        seen = seen + jnp.sum(part, axis=1, keepdims=True)
    rank = jnp.concatenate(ranks, axis=1).astype(jnp.int32)
    rank_hit = lax.broadcasted_iota(jnp.int32, (256, count), 0) == rank

    def collect(value):
        picked = jnp.where(rank_hit, value.astype(jnp.float32), 0.0).astype(jnp.bfloat16)
        return dot(owner_one, picked, NT)

    filled = collect(jnp.ones((1, count), jnp.int32)) > 0.5
    local_at = collect(local // 256) * 256.0 + collect(local % 256)
    source_at = collect(source // 16384) * 16384.0 + collect((source // 128) % 128) * 128.0 + collect(source % 128)
    ids_at = jnp.where(filled, local_at, -1.0).astype(jnp.int32)
    sources_at = jnp.where(filled, source_at, -1.0).astype(jnp.int32)
    pos = jnp.concatenate([owner * cap + rank, owner * packed_rows(cap) + rank], axis=0)
    return pos, ids_at, sources_at


def front_kernel(lists_dev, cap, x_hbm, list_hbm, source_hbm, table_hbm, tri_ref, pos_ref, got_ref, count_ref,
                 x_ref, list_ref, source_ref, table_ref, load_s, dest, part, core_buf, first_buf, sum_buf, second_buf, mid_sum, tile_buf, tally, tally_buf,
                 core_s, core_r, first_s, first_r, second_s, second_r, tile_s, tile_r, top_s, top_r, odd_s, odd_r,
                 fan_s, fan_r, row_s, row_r, pair_s, pair_r, wide_s, wide_r, id_s, id_r, tally_s, tally_r):
    z = lax.axis_index("group")
    dev = lax.axis_index("dev")
    owners = 32
    x, y, c = dev // 8, (dev // 2) % 4, dev % 2

    def at(xx, yy):
        return (z, (xx * 4 + yy) * 2 + c)

    other = (z, dev + 1 - 2 * c)
    along_x = [at((x + d) % 4, y) for d in (1, 2, 3)]
    along_y = [at(x, (y + d) % 4) for d in (1, 2, 3)]
    along_z = [((z + d) % 8, dev) for d in range(1, 8)]
    barrier = pltpu.get_barrier_semaphore()
    for k in range(1, owners):
        pl.semaphore_signal(barrier, inc=1, device_id=(z, (dev + k) % owners), device_id_type=MESH)
    for peer in along_z:
        pl.semaphore_signal(barrier, inc=1, device_id=peer, device_id_type=MESH)

    loads = [
        pltpu.make_async_copy(list_hbm, list_ref, load_s.at[4]),
        pltpu.make_async_copy(source_hbm, source_ref, load_s.at[5]),
        pltpu.make_async_copy(table_hbm, table_ref, load_s.at[6]),
    ]
    for k in range(4):
        columns = pl.ds(k * 256, 256)
        loads.append(pltpu.make_async_copy(x_hbm.at[:, columns], x_ref.at[:, columns], load_s.at[k]))
    for load in loads[3:] + loads[:3]:
        load.start()
    sent = []

    def copy_to(src, dst, s, r, peer):
        return pltpu.make_async_remote_copy(src_ref=src, dst_ref=dst, send_sem=s, recv_sem=r, device_id=peer,
                                            device_id_type=MESH)

    def send(src, dst, s, r, peer):
        copy = copy_to(src, dst, s, r, peer)
        copy.start()
        sent.append(copy)
        return copy

    def span(start, size):
        return pl.ds(pl.multiple_of(start, 8), size)

    lefts = {}

    def moment(pairs):
        for i, j in pairs:
            if i not in lefts:
                loads[3 + i].wait()
                lefts[i] = x_ref[:, i * 256:(i + 1) * 256].T
            square = dot(lefts[i], x_ref[:, j * 256:(j + 1) * 256])
            for a in range(2):
                for b in range(2):
                    key = (2 * i + a, 2 * j + b)
                    if key in STARTS:
                        begin = STARTS[key]
                        part[begin:begin + 128, :] = square[a * 128:(a + 1) * 128, b * 128:(b + 1) * 128]

    base = [p * 2 * HALF + c * HALF for p in range(2)]
    firsts = [(x, along_x), (y, along_y)]
    seconds = [(y, along_y), (x, along_x)]
    core = [None, None]
    first = [{}, {}]

    def swap(p):
        core[p] = send(part.at[span(p * 2 * HALF + (1 - c) * HALF, HALF)], core_buf.at[p], core_s.at[p], core_r.at[p],
                       other)

    def down_first(p):
        core[p].wait_recv()
        core_buf[p] = core_buf[p] + part[span(base[p], HALF), :]
        f, peers = firsts[p]
        s = seconds[p][0]
        for k in range(4):
            for d in (1, 2, 3):
                begin = ((f + d) % 4) * MID + ((s + 1 + k) % 4) * LOW
                first[p][k, d] = send(core_buf.at[p, span(begin, LOW)], first_buf.at[p, d - 1, k],
                                      first_s.at[p, d - 1, k], first_r.at[p, d - 1, k], peers[d - 1])

    moment(PAIRS[:5])
    pl.semaphore_wait(barrier, 38)
    swap(0)
    moment(PAIRS[5:8])
    down_first(0)
    moment(PAIRS[8:])
    swap(1)
    down_first(1)
    for load in loads[:3]:
        load.wait()
    pos, ids_at, sources_at = place_rows(list_ref[...], source_ref[...], table_ref[...], owners, lists_dev, cap)
    pos_ref[...] = pos
    dest[:, 0, :] = ids_at[:, :128]
    dest[:, 1, :] = ids_at[:, 128:]
    dest[:, 2, :] = sources_at[:, :128]
    dest[:, 3, :] = sources_at[:, 128:]
    second = [{}, {}]
    for k in range(4):
        for p in range(2):
            f = firsts[p][0]
            s, peers = seconds[p]
            for d in (1, 2, 3):
                first[p][k, d].wait_recv()
            own = core_buf[p, span(f * MID + ((s + 1 + k) % 4) * LOW, LOW), :]
            sum_buf[p, k] = (own + first_buf[p, 0, k]) + (first_buf[p, 1, k] + first_buf[p, 2, k])
            if k < 3:
                second[p][k] = send(sum_buf.at[p, k], second_buf.at[p, k], second_s.at[p, k], second_r.at[p, k], peers[k])
    tile = [[], []]
    for p in range(2):
        for k in range(3):
            second[p][k].wait_recv()
        mid_sum[p] = (sum_buf[p, 3] + second_buf[p, 0]) + (second_buf[p, 1] + second_buf[p, 2])
        for d in range(1, 8):
            tile[p].append(send(mid_sum.at[p, span(((z + d) % 8) * 8, 16)], tile_buf.at[p, d - 1],
                                tile_s.at[p, d - 1], tile_r.at[p, d - 1], along_z[d - 1]))
    arrive = []
    for k in range(1, owners):
        peer = (dev + k) % owners
        arrive.append(send(dest.at[peer], got_ref.at[dev], id_s.at[k - 1], id_r.at[k - 1], (z, peer)))
    got_ref[dev] = dest[dev]
    def hand(begin, size, s, r, peer):
        return send(tri_ref.at[span(begin, size)], tri_ref.at[span(begin, size)], s, r, peer)

    top = [[], []]

    def odd(p, d):
        begin = base[p] + firsts[p][0] * MID + seconds[p][0] * LOW + 64
        return copy_to(tri_ref.at[span(begin, 8)], tri_ref.at[span(begin, 8)], odd_s.at[p, d - 1], odd_r.at[p],
                       along_z[d - 1])

    for p in range(2):
        for copy in tile[p]:
            copy.wait_recv()
        total = mid_sum[p, span(z * 8, 16), :]
        for d in range(7):
            total = total + tile_buf[p, d]
        begin = base[p] + firsts[p][0] * MID + seconds[p][0] * LOW
        tri_ref[span(begin + z * 8, 8), :] = total[:8]
        for d in range(1, 8):
            top[p].append(hand(begin + z * 8, 8, top_s.at[p, d - 1], top_r.at[p, d - 1], along_z[d - 1]))

        @pl.when(z == 7)
        def _():
            tri_ref[span(begin + 64, 8), :] = total[8:]
            for d in range(1, 8):
                odd(p, d).start()

    for copy in arrive:
        copy.wait_recv()
    ids = jnp.concatenate([got_ref[:, 0, :], got_ref[:, 1, :]], axis=0)
    ids = jnp.concatenate([ids[k:k + 1, :] for k in range(2 * owners)], axis=1)
    count = ids.shape[1]
    high = lax.broadcasted_iota(jnp.int32, (16, count), 0) == jnp.where(ids >= 0, ids // 128, -1)
    low = lax.broadcasted_iota(jnp.int32, (128, count), 0) == ids % 128
    tally[...] = dot(narrow(high), narrow(low), NT)
    tallies = [send(tally, tally_buf.at[d - 1], tally_s.at[d - 1], tally_r.at[d - 1], along_z[d - 1])
               for d in range(1, 8)]

    fan = [{}, {}]
    row = [{}, {}]
    pair = [[], []]

    def outward(p, k):
        f, peers = firsts[p]
        begin = base[p] + f * MID + ((seconds[p][0] - k + 4) % 4) * LOW
        for d in (1, 2, 3):
            row[p][k, d] = hand(begin, LOW, row_s.at[p, k, d - 1], row_r.at[p, k, d - 1], peers[d - 1])
        pair[p].append(hand(begin, LOW, pair_s.at[p, k], pair_r.at[p, k], other))

    for p in range(2):
        for copy in top[p]:
            copy.wait_recv()

        @pl.when(z != 7)
        def _():
            odd(p, 1).wait_recv()

        s, peers = seconds[p]
        begin = base[p] + firsts[p][0] * MID + s * LOW
        for d in (1, 2, 3):
            fan[p][d] = hand(begin, LOW, fan_s.at[p, d - 1], fan_r.at[p, d - 1], peers[d - 1])
        outward(p, 0)
    for d in (1, 2, 3):
        for p in range(2):
            fan[p][d].wait_recv()
            outward(p, d)
    total = tally[...]
    for d in range(7):
        tallies[d].wait_recv()
        total = total + tally_buf[d]
    count_ref[...] = total.astype(jnp.int32)
    wide = [[], []]
    for d in (1, 2, 3):
        for p in range(2):
            for k in range(4):
                row[p][k, d].wait_recv()
            begin = base[p] + ((firsts[p][0] - d + 4) % 4) * MID
            wide[p].append(hand(begin, MID, wide_s.at[p, d - 1], wide_r.at[p, d - 1], other))
    for p in range(2):
        for copy in pair[p] + wide[p]:
            copy.wait_recv()
    for copy in sent:
        copy.wait_send()

    @pl.when(z == 7)
    def _():
        for p in range(2):
            for d in range(1, 8):
                odd(p, d).wait_send()


def front(corpus_rows, list_ids, source_ids, list_slot, owners, lists_dev, cap):
    count = list_ids.shape[0]
    sem = pltpu.SemaphoreType.DMA
    f32 = jnp.float32
    return pl.pallas_call(
        functools.partial(front_kernel, lists_dev, cap),
        out_shape=(
            jax.ShapeDtypeStruct((4 * HALF, 128), f32),
            jax.ShapeDtypeStruct((2, count), jnp.int32),
            jax.ShapeDtypeStruct((owners, 4, 128), jnp.int32),
            jax.ShapeDtypeStruct((lists_dev // 128, 128), jnp.int32),
        ),
        in_specs=[pl.BlockSpec(memory_space=pl.ANY)] * 4,
        out_specs=(vmem(),) * 4,
        scratch_shapes=[
            pltpu.VMEM(corpus_rows.shape, jnp.bfloat16),
            pltpu.VMEM((1, count), jnp.int32),
            pltpu.VMEM((1, count), jnp.int32),
            pltpu.VMEM((list_slot.shape[0] // 128, 128), jnp.int32),
            sem((7,)),
            pltpu.VMEM((owners, 4, 128), jnp.int32),
            pltpu.VMEM((4 * HALF, 128), f32),
            pltpu.VMEM((2, HALF, 128), f32),
            pltpu.VMEM((2, 3, 4, LOW, 128), f32),
            pltpu.VMEM((2, 4, LOW, 128), f32),
            pltpu.VMEM((2, 3, LOW, 128), f32),
            pltpu.VMEM((2, LOW, 128), f32),
            pltpu.VMEM((2, 7, 16, 128), f32),
            pltpu.VMEM((16, 128), f32),
            pltpu.VMEM((7, 16, 128), f32),
            sem((2,)), sem((2,)), sem((2, 3, 4)), sem((2, 3, 4)), sem((2, 3)), sem((2, 3)), sem((2, 7)), sem((2, 7)),
            sem((2, 7)), sem((2, 7)), sem((2, 7)), sem((2,)), sem((2, 3)), sem((2, 3)), sem((2, 4, 3)), sem((2, 4, 3)),
            sem((2, 4)), sem((2, 4)), sem((2, 3)), sem((2, 3)), sem((31,)), sem((31,)), sem((7,)), sem((7,)),
        ],
        compiler_params=pltpu.CompilerParams(collective_id=0, has_side_effects=True, vmem_limit_bytes=60 * 2**20),
        cost_estimate=pl.CostEstimate(flops=10**10, bytes_accessed=10**8, transcendentals=0),
        name="front",
    )(corpus_rows, list_ids.reshape(1, count), source_ids.reshape(1, count), list_slot.reshape(-1, 128))


def step_of(exponent):
    return jnp.exp2((exponent - 23).astype(jnp.float32))


def project_rows(rows_ref, basis_ref, z_ref):
    count = rows_ref.shape[0]
    width = basis_ref.shape[1] // 2
    step = 1024
    for begin in range(0, count, step):
        both = dot(rows_ref[begin:begin + step, :], basis_ref[...])
        code = both[:, :width] + both[:, width:]
        z_ref[begin:begin + step, :] = code[:, :128]
        z_ref[count + begin:count + begin + step, :] = code[:, 128:]


def project_kernel(cap, tri_ref, start_ref, x_hbm, pos_ref, out_ref, basis_ref, gram_ref, x_ref, load_s, m_hi, m_lo,
                   z_ref, word_ref, tail_ref, sent_ref):
    load = pltpu.make_async_copy(x_hbm, x_ref, load_s)
    load.start()
    eye = lax.broadcasted_iota(jnp.int32, (128, 128), 0) == lax.broadcasted_iota(jnp.int32, (128, 128), 1)
    peak = jnp.zeros((128, 128), jnp.float32)
    for i in range(8):
        for j in range(i + 1):
            at = STARTS[(i, j)]
            block = tri_ref[at:at + 128, :]
            hi, lo = halves(block)
            m_hi[i * 128:(i + 1) * 128, j * 128:(j + 1) * 128] = hi
            m_lo[i * 128:(i + 1) * 128, j * 128:(j + 1) * 128] = lo
            if i != j:
                hi, lo = halves(block.T)
                m_hi[j * 128:(j + 1) * 128, i * 128:(i + 1) * 128] = hi
                m_lo[j * 128:(j + 1) * 128, i * 128:(i + 1) * 128] = lo
            else:
                peak = jnp.maximum(peak, jnp.where(eye, block, 0.0))
    scale = 1.0 / jnp.max(jnp.max(peak, axis=0, keepdims=True), axis=1, keepdims=True)
    width = start_ref.shape[1]

    def times_moment(v):
        hi, lo = halves(v * scale)
        both = dot(m_hi[...], jnp.concatenate([hi, lo], axis=1))
        return (both[:, :width] + both[:, width:]) + dot(m_lo[...], hi)

    product = times_moment(times_moment(start_ref[...]))
    product = product * lax.rsqrt(jnp.sum(product * product, axis=0, keepdims=True))
    hi, lo = halves(product)
    basis_ref[:, :width] = hi
    basis_ref[:, width:] = lo
    cross = dot(hi, basis_ref[...], TN)
    mixed = cross[:, width:]
    gram_ref[...] = cross[:, :width] + (mixed + mixed.T)
    load.wait()
    project_rows(x_ref, basis_ref, z_ref)
    count = x_ref.shape[0]

    peak = jnp.max(jnp.max(jnp.abs(z_ref[...]), axis=0, keepdims=True), axis=1, keepdims=True)
    lane = lax.broadcasted_iota(jnp.int32, (1, 128), 1)
    below = jnp.where(peak >= jnp.exp2((lane - 64).astype(jnp.float32)), 1.0, 0.0)
    exponent = jnp.sum(below, axis=1, keepdims=True).astype(jnp.int32) - 64
    unit = 1.0 / step_of(exponent)
    most = float(2**23 - 1)
    step = 256

    @pl.loop(0, count // step)
    def _(k):
        at = pl.multiple_of(k * step, step)

        def coded(begin):
            return jnp.clip(jnp.round(z_ref[pl.ds(begin, step), :] * unit), -most, most).astype(jnp.int32)

        low = coded(at)
        high = coded(pl.multiple_of(at + count, step))
        word_ref[pl.ds(at, step), :] = (low << 8) | (high & 255)
        upper = high >> 8
        tail_ref[pl.ds(at, step), :] = (upper << 16) | (pltpu.roll(upper, 64, 1) & 65535)

    @pl.loop(0, count // 16)
    def _(k):
        for u in range(16):
            row = k * 16 + u
            out_ref[pl.ds(pos_ref[1, row], 1), :] = word_ref[pl.ds(row, 1), :]
            sent_ref[pl.ds(pos_ref[0, row], 1), :] = tail_ref[pl.ds(row, 1), :]

    half = cap // 2
    left = lax.broadcasted_iota(jnp.int32, (half, 128), 1) < 64
    for owner in range(sent_ref.shape[0] // cap):
        begin = owner * packed_rows(cap) + cap
        first = sent_ref[owner * cap:owner * cap + half, :]
        second = sent_ref[owner * cap + half:(owner + 1) * cap, :]
        out_ref[begin:begin + half, :] = jnp.where(left, first, pltpu.roll(second, 64, 1))
        out_ref[begin + half:begin + half + 8, :] = jnp.broadcast_to(exponent, (8, 128))


def project(tri, start, x, pos, owners, cap):
    feature, width = start.shape
    return pl.pallas_call(
        functools.partial(project_kernel, cap),
        out_shape=(
            jax.ShapeDtypeStruct((owners * packed_rows(cap), 128), jnp.int32),
            jax.ShapeDtypeStruct((feature, 2 * width), jnp.bfloat16),
            jax.ShapeDtypeStruct((width, width), jnp.float32),
        ),
        in_specs=[vmem(), vmem(), pl.BlockSpec(memory_space=pl.ANY), smem()],
        out_specs=(vmem(), vmem(), vmem()),
        scratch_shapes=[
            pltpu.VMEM(x.shape, jnp.bfloat16),
            pltpu.SemaphoreType.DMA,
            pltpu.VMEM((feature, feature), jnp.bfloat16),
            pltpu.VMEM((feature, feature), jnp.bfloat16),
            pltpu.VMEM((2 * x.shape[0], 128), jnp.float32),
            pltpu.VMEM((x.shape[0], 128), jnp.int32),
            pltpu.VMEM((x.shape[0], 128), jnp.int32),
            pltpu.VMEM((owners * cap, 128), jnp.int32),
        ],
        compiler_params=limits(),
        cost_estimate=pl.CostEstimate(flops=10**10, bytes_accessed=2 * 10**7, transcendentals=0),
        name="project",
    )(tri, start, x, pos)


def factor_kernel(gram_ref, inverse_ref, pivot_ref, aug):
    size = gram_ref.shape[0]
    block = 32
    panel = 8
    aug[:, :size] = gram_ref[...]
    aug[:, size:] = (
        lax.broadcasted_iota(jnp.int32, (size, size), 0) == lax.broadcasted_iota(jnp.int32, (size, size), 1)
    ).astype(jnp.float32)
    row_at = lax.broadcasted_iota(jnp.int32, (block, 128), 0)
    lane_at = lax.broadcasted_iota(jnp.int32, (block, 128), 1)
    least = jnp.full((1, 128), 1e30, jnp.float32)
    for b in range(size // block):
        lo, hi = b * block, (b + 1) * block
        square = aug[lo:hi, lo:hi]
        unit = (row_at[:, :block] == lane_at[:, :block]).astype(jnp.float32)
        work = jnp.concatenate([square, unit, jnp.zeros((block, 128 - 2 * block), jnp.float32)], axis=1)
        for p in range(block // panel):
            cols = [
                jnp.broadcast_to(work[:, p * panel + j:p * panel + j + 1], (block, 128)) for j in range(panel)
            ]
            for j in range(panel):
                k = p * panel + j
                pivot = cols[j][k:k + 1, :]
                least = jnp.minimum(least, pivot)
                root = lax.rsqrt(pivot)
                column = jnp.where(row_at > k, cols[j] * root, 0.0)
                for jj in range(j + 1, panel):
                    kk = p * panel + jj
                    cols[jj] = cols[jj] - column * column[kk:kk + 1, :]
                row = work[k:k + 1, :] * root
                work = jnp.where(row_at == k, row, work - column * row)
        inverse = work[:, block:2 * block]
        rows = lax.dot_general(inverse, aug[lo:hi, :], (((1,), (0,)), ((), ())), precision=lax.Precision.HIGHEST,
                               preferred_element_type=jnp.float32)
        aug[lo:hi, :] = rows
        if hi < size:
            below = rows[:, hi:size].T
            aug[hi:, :] -= lax.dot_general(below, rows, (((1,), (0,)), ((), ())), precision=lax.Precision.HIGHEST,
                                           preferred_element_type=jnp.float32)
    whole = aug[:, size:].T
    top, bottom = halves(whole)
    inverse_ref[:, :size] = top
    inverse_ref[:, size:] = bottom
    pivot_ref[...] = least


def factor(gram):
    size = gram.shape[0]
    return pl.pallas_call(
        factor_kernel,
        out_shape=(
            jax.ShapeDtypeStruct((size, 2 * size), jnp.bfloat16),
            jax.ShapeDtypeStruct((1, 128), jnp.float32),
        ),
        in_specs=[vmem()],
        out_specs=(vmem(), vmem()),
        scratch_shapes=[pltpu.VMEM((size, 2 * size), jnp.float32)],
        compiler_params=limits(),
        cost_estimate=pl.CostEstimate(flops=10**9, bytes_accessed=10**7, transcendentals=0),
        name="factor",
    )(gram)


def offset_kernel(cap, c_ref, basis_ref, id_ref, out_ref, z_ref):
    project_rows(c_ref, basis_ref, z_ref)
    count = c_ref.shape[0]

    @pl.loop(0, id_ref.shape[0] // cap)
    def _(sender):
        @pl.loop(0, cap // 16)
        def _(k):
            for u in range(16):
                rank = k * 16 + u
                row = jnp.maximum(id_ref[sender * cap + rank], 0)
                slot = sender * (2 * cap) + rank
                out_ref[pl.ds(slot, 1), :] = z_ref[pl.ds(row, 1), :]
                out_ref[pl.ds(slot + cap, 1), :] = z_ref[pl.ds(row + count, 1), :]


def offsets_at(centroids, basis, ids, cap):
    return pl.pallas_call(
        functools.partial(offset_kernel, cap),
        out_shape=jax.ShapeDtypeStruct((2 * ids.shape[0], 128), jnp.float32),
        in_specs=[vmem(), vmem(), smem()],
        out_specs=vmem(),
        scratch_shapes=[pltpu.VMEM((2 * centroids.shape[0], 128), jnp.float32)],
        compiler_params=limits(),
        cost_estimate=pl.CostEstimate(flops=10**10, bytes_accessed=10**7, transcendentals=0),
        name="offsets",
    )(centroids, basis, ids)


def finish_kernel(senders, z_ref, off_ref, count_ref, inverse_ref, out_ref):
    width = out_ref.shape[1]
    cap = out_ref.shape[0] // senders
    rank = lax.broadcasted_iota(jnp.int32, (cap, width), 0)
    half = cap // 2
    left = lax.broadcasted_iota(jnp.int32, (half, 128), 1) < 64
    gaps = []
    for s in range(senders):
        begin = s * packed_rows(cap)
        word = z_ref[begin:begin + cap, :]
        tail = z_ref[begin + cap:begin + cap + half, :]
        unit = step_of(z_ref[begin + cap + half:begin + cap + half + 1, :])
        upper = tail >> 16
        under = (tail << 16) >> 16
        first = jnp.where(left, upper, pltpu.roll(under, 64, 1))
        second = jnp.where(left, pltpu.roll(upper, 64, 1), under)
        high = (jnp.concatenate([first, second], axis=0) << 8) | (word & 255)
        begin = 2 * s * cap
        low = (word >> 8).astype(jnp.float32) * unit - off_ref[begin:begin + cap, :]
        high = high.astype(jnp.float32) * unit - off_ref[begin + cap:begin + 2 * cap, :]
        gaps.append(jnp.concatenate([low, high], axis=1))
    hi, lo = halves(jnp.concatenate(gaps, axis=0))
    both = dot(hi, inverse_ref[...])
    code = (both[:, :width] + both[:, width:]) + dot(lo, inverse_ref[:, :width])
    for s in range(senders):
        filled = rank < count_ref[pl.program_id(0) * senders + s]
        at = slice(s * cap, (s + 1) * cap)
        out_ref[at, :] = jnp.where(filled, code[at, :], 0.0).astype(jnp.bfloat16)


def finish(z, off, filled, inverse):
    owners = filled.shape[0]
    slots = off.shape[0] // 2
    width = inverse.shape[0]
    senders = 4
    step = senders * (slots // owners)
    return pl.pallas_call(
        functools.partial(finish_kernel, senders),
        out_shape=jax.ShapeDtypeStruct((slots, width), jnp.bfloat16),
        grid=(slots // step,),
        in_specs=[
            pl.BlockSpec((z.shape[0] // owners * senders, 128), lambda s: (s, 0)),
            pl.BlockSpec((2 * step, 128), lambda s: (s, 0)),
            smem(),
            pl.BlockSpec((width, 2 * width), lambda s: (0, 0)),
        ],
        out_specs=pl.BlockSpec((step, width), lambda s: (s, 0)),
        compiler_params=limits(),
        cost_estimate=pl.CostEstimate(flops=2 * 10**9, bytes_accessed=13 * 10**6, transcendentals=0),
        name="finish",
    )(z, off, filled, inverse)


exact_mode = lax.Precision.HIGHEST
PIVOT_LEAST = 1.0 / 64.0


def orthonormal(product):
    gram_matrix = jnp.dot(product.T, product, precision=exact_mode, preferred_element_type=jnp.float32)
    lower = jnp.linalg.cholesky(gram_matrix)
    return jax.scipy.linalg.solve_triangular(lower, product.T, lower=True).T


def careful(tri, start, x, centroids, pos, ids):
    owners = lax.axis_size("dev")
    slots = ids.shape[0]
    grid = [[None] * 8 for _ in range(8)]
    for i in range(8):
        for j in range(i + 1):
            at = STARTS[(i, j)]
            grid[i][j] = tri[at:at + 128]
            grid[j][i] = tri[at:at + 128].T
    moment = jnp.block(grid)
    basis = start
    for sweep in range(2):
        product = jnp.dot(moment, basis, precision=exact_mode, preferred_element_type=jnp.float32)
        basis = orthonormal(product)
    width = start.shape[1]
    projected = jnp.dot(x, basis, precision=exact_mode, preferred_element_type=jnp.float32)
    sent = jnp.zeros((slots, width), jnp.float32).at[pos[0]].set(projected)
    sent = sent.reshape(owners, slots // owners, width)
    values = lax.all_to_all(sent, "dev", split_axis=0, concat_axis=0, tiled=True).reshape(slots, width)
    offsets = jnp.dot(centroids, basis, precision=exact_mode, preferred_element_type=jnp.float32)
    code = values - jnp.take(offsets, jnp.maximum(ids, 0), axis=0)
    return jnp.where(ids[:, None] >= 0, code, 0.0).astype(jnp.bfloat16)


def shards(corpus_rows, list_ids, source_ids, list_slot, centroids, start_basis):
    owners = lax.axis_size("dev")
    lists_dev = centroids.shape[0]
    slots = owners * CAP
    tri, pos, arrived, counts = front(corpus_rows, list_ids, source_ids, list_slot, owners, lists_dev, CAP)
    sent, basis, gram = project(tri, start_basis, corpus_rows, pos, owners, CAP)
    values = lax.all_to_all(
        sent.reshape(owners, packed_rows(CAP), 128), "dev", split_axis=0, concat_axis=0, tiled=True
    ).reshape(owners * packed_rows(CAP), 128)
    ids = arrived[:, :2].reshape(owners, 256)[:, :CAP]
    filled = jnp.sum((ids >= 0).astype(jnp.int32), axis=1)
    ids = ids.reshape(slots)
    row_sources = arrived[:, 2:].reshape(owners, 256)[:, :CAP].reshape(slots)
    inverse, pivots = factor(gram)
    off = offsets_at(centroids, basis, ids, CAP)
    row_codes = lax.cond(
        jnp.min(pivots) >= PIVOT_LEAST,
        lambda codes: codes,
        lambda codes: careful(tri, start_basis, corpus_rows, centroids, pos, ids),
        finish(values, off, filled, inverse),
    )
    return row_codes, row_sources, counts.reshape(lists_dev)


def solution(mesh):
    placed = (
        P(("group", "dev"), None),
        P(("group", "dev")),
        P(("group", "dev")),
        P(),
        P("dev", None),
        P(),
    )
    return jax.shard_map(
        shards,
        mesh=mesh,
        in_specs=placed,
        out_specs=(P(("group", "dev"), None), P(("group", "dev")), P("dev")),
        check_vma=False,
    )
```

```python
import functools
import jax
import jax.numpy as jnp
from jax import lax
from jax.experimental import pallas as pl
from jax.experimental.pallas import tpu as pltpu
from jax.sharding import PartitionSpec as P

CAP = 160
MESH = pl.DeviceIdType.MESH
NT = (((1,), (1,)), ((), ()))
TN = (((0,), (0,)), ((), ()))
HALF, MID, LOW = 1152, 288, 72
PAIRS = ((0, 0), (1, 0), (1, 1), (2, 0), (2, 1), (2, 2), (3, 0), (3, 1), (3, 2), (3, 3))


def block_starts():
    starts = {}
    for i, j in PAIRS:
        for a in range(2):
            for b in range(2):
                if 2 * j + b <= 2 * i + a:
                    starts[(2 * i + a, 2 * j + b)] = len(starts) * 128
    return starts


STARTS = block_starts()


def vmem():
    return pl.BlockSpec(memory_space=pltpu.VMEM)


def smem():
    return pl.BlockSpec(memory_space=pltpu.SMEM)


def limits():
    return pltpu.CompilerParams(vmem_limit_bytes=48 * 2**20)


def halves(v):
    top = v.astype(jnp.bfloat16)
    return top, (v - top.astype(jnp.float32)).astype(jnp.bfloat16)


def dot(a, b, dims=(((1,), (0,)), ((), ()))):
    return lax.dot_general(a, b, dims, preferred_element_type=jnp.float32)


def packed_rows(cap):
    return cap + cap // 2 + 8


def narrow(flag):
    return flag.astype(jnp.float32).astype(jnp.bfloat16)


def place_rows(ids, source, table, owners, lists_dev, cap):
    count = ids.shape[1]
    sub = lax.broadcasted_iota(jnp.int32, (table.shape[0], count), 0)
    row_hit = narrow(sub == ids // 128)
    high = dot((table // 256).astype(jnp.float32).astype(jnp.bfloat16), row_hit, TN)
    low = dot((table % 256).astype(jnp.float32).astype(jnp.bfloat16), row_hit, TN)
    lane = lax.broadcasted_iota(jnp.int32, (128, count), 0)
    slot = jnp.sum(jnp.where(lane == ids % 128, high * 256.0 + low, 0.0), axis=0, keepdims=True).astype(jnp.int32)
    owner = slot // lists_dev
    local = slot % lists_dev
    owner_one = narrow(lax.broadcasted_iota(jnp.int32, (owners, count), 0) == owner)
    width = 256
    square = (width, width)
    before = narrow(lax.broadcasted_iota(jnp.int32, square, 0) < lax.broadcasted_iota(jnp.int32, square, 1))
    seen = jnp.zeros((owners, 1), jnp.float32)
    ranks = []
    for k in range(count // width):
        part = owner_one[:, k * width:(k + 1) * width]
        prior = dot(part, before) + seen
        part = part.astype(jnp.float32)
        ranks.append(jnp.sum(prior * part, axis=0, keepdims=True))
        seen = seen + jnp.sum(part, axis=1, keepdims=True)
    rank = jnp.concatenate(ranks, axis=1).astype(jnp.int32)
    rank_hit = lax.broadcasted_iota(jnp.int32, (256, count), 0) == rank

    def collect(value):
        picked = jnp.where(rank_hit, value.astype(jnp.float32), 0.0).astype(jnp.bfloat16)
        return dot(owner_one, picked, NT)

    filled = collect(jnp.ones((1, count), jnp.int32)) > 0.5
    local_at = collect(local // 256) * 256.0 + collect(local % 256)
    source_at = collect(source // 16384) * 16384.0 + collect((source // 128) % 128) * 128.0 + collect(source % 128)
    ids_at = jnp.where(filled, local_at, -1.0).astype(jnp.int32)
    sources_at = jnp.where(filled, source_at, -1.0).astype(jnp.int32)
    pos = jnp.concatenate([owner * cap + rank, owner * packed_rows(cap) + rank], axis=0)
    return pos, ids_at, sources_at


def front_kernel(lists_dev, cap, x_hbm, list_hbm, source_hbm, table_hbm, tri_ref, pos_ref, got_ref, count_ref,
                 x_ref, list_ref, source_ref, table_ref, load_s, dest, part, core_buf, first_buf, sum_buf, second_buf, mid_sum, tile_buf, tally, tally_buf,
                 core_s, core_r, first_s, first_r, second_s, second_r, tile_s, tile_r, top_s, top_r, odd_s, odd_r,
                 fan_s, fan_r, row_s, row_r, pair_s, pair_r, wide_s, wide_r, id_s, id_r, tally_s, tally_r):
    z = lax.axis_index("group")
    dev = lax.axis_index("dev")
    owners = 32
    x, y, c = dev // 8, (dev // 2) % 4, dev % 2

    def at(xx, yy):
        return (z, (xx * 4 + yy) * 2 + c)

    other = (z, dev + 1 - 2 * c)
    along_x = [at((x + d) % 4, y) for d in (1, 2, 3)]
    along_y = [at(x, (y + d) % 4) for d in (1, 2, 3)]
    along_z = [((z + d) % 8, dev) for d in range(1, 8)]
    barrier = pltpu.get_barrier_semaphore()
    for k in range(1, owners):
        pl.semaphore_signal(barrier, inc=1, device_id=(z, (dev + k) % owners), device_id_type=MESH)
    for peer in along_z:
        pl.semaphore_signal(barrier, inc=1, device_id=peer, device_id_type=MESH)

    loads = [
        pltpu.make_async_copy(list_hbm, list_ref, load_s.at[4]),
        pltpu.make_async_copy(source_hbm, source_ref, load_s.at[5]),
        pltpu.make_async_copy(table_hbm, table_ref, load_s.at[6]),
    ]
    for k in range(4):
        columns = pl.ds(k * 256, 256)
        loads.append(pltpu.make_async_copy(x_hbm.at[:, columns], x_ref.at[:, columns], load_s.at[k]))
    for load in loads[3:] + loads[:3]:
        load.start()
    sent = []

    def copy_to(src, dst, s, r, peer):
        return pltpu.make_async_remote_copy(src_ref=src, dst_ref=dst, send_sem=s, recv_sem=r, device_id=peer,
                                            device_id_type=MESH)

    def send(src, dst, s, r, peer):
        copy = copy_to(src, dst, s, r, peer)
        copy.start()
        sent.append(copy)
        return copy

    def span(start, size):
        return pl.ds(pl.multiple_of(start, 8), size)

    lefts = {}

    def moment(pairs):
        for i, j in pairs:
            if i not in lefts:
                loads[3 + i].wait()
                lefts[i] = x_ref[:, i * 256:(i + 1) * 256].T
            square = dot(lefts[i], x_ref[:, j * 256:(j + 1) * 256])
            for a in range(2):
                for b in range(2):
                    key = (2 * i + a, 2 * j + b)
                    if key in STARTS:
                        begin = STARTS[key]
                        part[begin:begin + 128, :] = square[a * 128:(a + 1) * 128, b * 128:(b + 1) * 128]

    base = [p * 2 * HALF + c * HALF for p in range(2)]
    firsts = [(x, along_x), (y, along_y)]
    seconds = [(y, along_y), (x, along_x)]
    core = [None, None]
    first = [{}, {}]

    def swap(p):
        core[p] = send(part.at[span(p * 2 * HALF + (1 - c) * HALF, HALF)], core_buf.at[p], core_s.at[p], core_r.at[p],
                       other)

    def down_first(p):
        core[p].wait_recv()
        core_buf[p] = core_buf[p] + part[span(base[p], HALF), :]
        f, peers = firsts[p]
        s = seconds[p][0]
        for k in range(4):
            for d in (1, 2, 3):
                begin = ((f + d) % 4) * MID + ((s + 1 + k) % 4) * LOW
                first[p][k, d] = send(core_buf.at[p, span(begin, LOW)], first_buf.at[p, d - 1, k],
                                      first_s.at[p, d - 1, k], first_r.at[p, d - 1, k], peers[d - 1])

    moment(PAIRS[:5])
    pl.semaphore_wait(barrier, 38)
    swap(0)
    moment(PAIRS[5:8])
    down_first(0)
    moment(PAIRS[8:])
    swap(1)
    down_first(1)
    for load in loads[:3]:
        load.wait()
    pos, ids_at, sources_at = place_rows(list_ref[...], source_ref[...], table_ref[...], owners, lists_dev, cap)
    pos_ref[...] = pos
    dest[:, 0, :] = ids_at[:, :128]
    dest[:, 1, :] = ids_at[:, 128:]
    dest[:, 2, :] = sources_at[:, :128]
    dest[:, 3, :] = sources_at[:, 128:]
    second = [{}, {}]
    for k in range(4):
        for p in range(2):
            f = firsts[p][0]
            s, peers = seconds[p]
            for d in (1, 2, 3):
                first[p][k, d].wait_recv()
            own = core_buf[p, span(f * MID + ((s + 1 + k) % 4) * LOW, LOW), :]
            sum_buf[p, k] = (own + first_buf[p, 0, k]) + (first_buf[p, 1, k] + first_buf[p, 2, k])
            if k < 3:
                second[p][k] = send(sum_buf.at[p, k], second_buf.at[p, k], second_s.at[p, k], second_r.at[p, k], peers[k])
    tile = [[], []]
    for p in range(2):
        for k in range(3):
            second[p][k].wait_recv()
        mid_sum[p] = (sum_buf[p, 3] + second_buf[p, 0]) + (second_buf[p, 1] + second_buf[p, 2])
        for d in range(1, 8):
            tile[p].append(send(mid_sum.at[p, span(((z + d) % 8) * 8, 16)], tile_buf.at[p, d - 1],
                                tile_s.at[p, d - 1], tile_r.at[p, d - 1], along_z[d - 1]))
    arrive = []
    for k in range(1, owners):
        peer = (dev + k) % owners
        arrive.append(send(dest.at[peer], got_ref.at[dev], id_s.at[k - 1], id_r.at[k - 1], (z, peer)))
    got_ref[dev] = dest[dev]
    def hand(begin, size, s, r, peer):
        return send(tri_ref.at[span(begin, size)], tri_ref.at[span(begin, size)], s, r, peer)

    top = [[], []]

    def odd(p, d):
        begin = base[p] + firsts[p][0] * MID + seconds[p][0] * LOW + 64
        return copy_to(tri_ref.at[span(begin, 8)], tri_ref.at[span(begin, 8)], odd_s.at[p, d - 1], odd_r.at[p],
                       along_z[d - 1])

    for p in range(2):
        for copy in tile[p]:
            copy.wait_recv()
        total = mid_sum[p, span(z * 8, 16), :]
        for d in range(7):
            total = total + tile_buf[p, d]
        begin = base[p] + firsts[p][0] * MID + seconds[p][0] * LOW
        tri_ref[span(begin + z * 8, 8), :] = total[:8]
        for d in range(1, 8):
            top[p].append(hand(begin + z * 8, 8, top_s.at[p, d - 1], top_r.at[p, d - 1], along_z[d - 1]))

        @pl.when(z == 7)
        def _():
            tri_ref[span(begin + 64, 8), :] = total[8:]
            for d in range(1, 8):
                odd(p, d).start()

    for copy in arrive:
        copy.wait_recv()
    ids = jnp.concatenate([got_ref[:, 0, :], got_ref[:, 1, :]], axis=0)
    ids = jnp.concatenate([ids[k:k + 1, :] for k in range(2 * owners)], axis=1)
    count = ids.shape[1]
    high = lax.broadcasted_iota(jnp.int32, (16, count), 0) == jnp.where(ids >= 0, ids // 128, -1)
    low = lax.broadcasted_iota(jnp.int32, (128, count), 0) == ids % 128
    tally[...] = dot(narrow(high), narrow(low), NT)
    tallies = [send(tally, tally_buf.at[d - 1], tally_s.at[d - 1], tally_r.at[d - 1], along_z[d - 1])
               for d in range(1, 8)]

    fan = [{}, {}]
    row = [{}, {}]
    pair = [[], []]

    def outward(p, k):
        f, peers = firsts[p]
        begin = base[p] + f * MID + ((seconds[p][0] - k + 4) % 4) * LOW
        for d in (1, 2, 3):
            row[p][k, d] = hand(begin, LOW, row_s.at[p, k, d - 1], row_r.at[p, k, d - 1], peers[d - 1])
        pair[p].append(hand(begin, LOW, pair_s.at[p, k], pair_r.at[p, k], other))

    for p in range(2):
        for copy in top[p]:
            copy.wait_recv()

        @pl.when(z != 7)
        def _():
            odd(p, 1).wait_recv()

        s, peers = seconds[p]
        begin = base[p] + firsts[p][0] * MID + s * LOW
        for d in (1, 2, 3):
            fan[p][d] = hand(begin, LOW, fan_s.at[p, d - 1], fan_r.at[p, d - 1], peers[d - 1])
        outward(p, 0)
    for d in (1, 2, 3):
        for p in range(2):
            fan[p][d].wait_recv()
            outward(p, d)
    total = tally[...]
    for d in range(7):
        tallies[d].wait_recv()
        total = total + tally_buf[d]
    count_ref[...] = total.astype(jnp.int32)
    wide = [[], []]
    for d in (1, 2, 3):
        for p in range(2):
            for k in range(4):
                row[p][k, d].wait_recv()
            begin = base[p] + ((firsts[p][0] - d + 4) % 4) * MID
            wide[p].append(hand(begin, MID, wide_s.at[p, d - 1], wide_r.at[p, d - 1], other))
    for p in range(2):
        for copy in pair[p] + wide[p]:
            copy.wait_recv()
    for copy in sent:
        copy.wait_send()

    @pl.when(z == 7)
    def _():
        for p in range(2):
            for d in range(1, 8):
                odd(p, d).wait_send()


def front(corpus_rows, list_ids, source_ids, list_slot, owners, lists_dev, cap):
    count = list_ids.shape[0]
    sem = pltpu.SemaphoreType.DMA
    f32 = jnp.float32
    return pl.pallas_call(
        functools.partial(front_kernel, lists_dev, cap),
        out_shape=(
            jax.ShapeDtypeStruct((4 * HALF, 128), f32),
            jax.ShapeDtypeStruct((2, count), jnp.int32),
            jax.ShapeDtypeStruct((owners, 4, 128), jnp.int32),
            jax.ShapeDtypeStruct((lists_dev // 128, 128), jnp.int32),
        ),
        in_specs=[pl.BlockSpec(memory_space=pl.ANY)] * 4,
        out_specs=(vmem(),) * 4,
        scratch_shapes=[
            pltpu.VMEM(corpus_rows.shape, jnp.bfloat16),
            pltpu.VMEM((1, count), jnp.int32),
            pltpu.VMEM((1, count), jnp.int32),
            pltpu.VMEM((list_slot.shape[0] // 128, 128), jnp.int32),
            sem((7,)),
            pltpu.VMEM((owners, 4, 128), jnp.int32),
            pltpu.VMEM((4 * HALF, 128), f32),
            pltpu.VMEM((2, HALF, 128), f32),
            pltpu.VMEM((2, 3, 4, LOW, 128), f32),
            pltpu.VMEM((2, 4, LOW, 128), f32),
            pltpu.VMEM((2, 3, LOW, 128), f32),
            pltpu.VMEM((2, LOW, 128), f32),
            pltpu.VMEM((2, 7, 16, 128), f32),
            pltpu.VMEM((16, 128), f32),
            pltpu.VMEM((7, 16, 128), f32),
            sem((2,)), sem((2,)), sem((2, 3, 4)), sem((2, 3, 4)), sem((2, 3)), sem((2, 3)), sem((2, 7)), sem((2, 7)),
            sem((2, 7)), sem((2, 7)), sem((2, 7)), sem((2,)), sem((2, 3)), sem((2, 3)), sem((2, 4, 3)), sem((2, 4, 3)),
            sem((2, 4)), sem((2, 4)), sem((2, 3)), sem((2, 3)), sem((31,)), sem((31,)), sem((7,)), sem((7,)),
        ],
        compiler_params=pltpu.CompilerParams(collective_id=0, has_side_effects=True, vmem_limit_bytes=60 * 2**20),
        cost_estimate=pl.CostEstimate(flops=10**10, bytes_accessed=10**8, transcendentals=0),
        name="front",
    )(corpus_rows, list_ids.reshape(1, count), source_ids.reshape(1, count), list_slot.reshape(-1, 128))


def step_of(exponent):
    return jnp.exp2((exponent - 23).astype(jnp.float32))


def project_rows(rows_ref, basis_ref, z_ref):
    count = rows_ref.shape[0]
    width = basis_ref.shape[1] // 2
    step = 1024
    for begin in range(0, count, step):
        both = dot(rows_ref[begin:begin + step, :], basis_ref[...])
        code = both[:, :width] + both[:, width:]
        z_ref[begin:begin + step, :] = code[:, :128]
        z_ref[count + begin:count + begin + step, :] = code[:, 128:]


def project_kernel(cap, tri_ref, start_ref, x_hbm, pos_ref, out_ref, basis_ref, gram_ref, x_ref, load_s, m_hi, m_lo,
                   z_ref, word_ref, tail_ref, sent_ref):
    load = pltpu.make_async_copy(x_hbm, x_ref, load_s)
    load.start()
    eye = lax.broadcasted_iota(jnp.int32, (128, 128), 0) == lax.broadcasted_iota(jnp.int32, (128, 128), 1)
    peak = jnp.zeros((128, 128), jnp.float32)
    for i in range(8):
        for j in range(i + 1):
            at = STARTS[(i, j)]
            block = tri_ref[at:at + 128, :]
            hi, lo = halves(block)
            m_hi[i * 128:(i + 1) * 128, j * 128:(j + 1) * 128] = hi
            m_lo[i * 128:(i + 1) * 128, j * 128:(j + 1) * 128] = lo
            if i != j:
                hi, lo = halves(block.T)
                m_hi[j * 128:(j + 1) * 128, i * 128:(i + 1) * 128] = hi
                m_lo[j * 128:(j + 1) * 128, i * 128:(i + 1) * 128] = lo
            else:
                peak = jnp.maximum(peak, jnp.where(eye, block, 0.0))
    scale = 1.0 / jnp.max(jnp.max(peak, axis=0, keepdims=True), axis=1, keepdims=True)
    width = start_ref.shape[1]

    def times_moment(v):
        hi, lo = halves(v * scale)
        both = dot(m_hi[...], jnp.concatenate([hi, lo], axis=1))
        return (both[:, :width] + both[:, width:]) + dot(m_lo[...], hi)

    product = times_moment(times_moment(start_ref[...]))
    product = product * lax.rsqrt(jnp.sum(product * product, axis=0, keepdims=True))
    hi, lo = halves(product)
    basis_ref[:, :width] = hi
    basis_ref[:, width:] = lo
    cross = dot(hi, basis_ref[...], TN)
    mixed = cross[:, width:]
    gram_ref[...] = cross[:, :width] + (mixed + mixed.T)
    load.wait()
    project_rows(x_ref, basis_ref, z_ref)
    count = x_ref.shape[0]

    peak = jnp.max(jnp.max(jnp.abs(z_ref[...]), axis=0, keepdims=True), axis=1, keepdims=True)
    lane = lax.broadcasted_iota(jnp.int32, (1, 128), 1)
    below = jnp.where(peak >= jnp.exp2((lane - 64).astype(jnp.float32)), 1.0, 0.0)
    exponent = jnp.sum(below, axis=1, keepdims=True).astype(jnp.int32) - 64
    unit = 1.0 / step_of(exponent)
    most = float(2**23 - 1)
    step = 256

    @pl.loop(0, count // step)
    def _(k):
        at = pl.multiple_of(k * step, step)

        def coded(begin):
            return jnp.clip(jnp.round(z_ref[pl.ds(begin, step), :] * unit), -most, most).astype(jnp.int32)

        low = coded(at)
        high = coded(pl.multiple_of(at + count, step))
        word_ref[pl.ds(at, step), :] = (low << 8) | (high & 255)
        upper = high >> 8
        tail_ref[pl.ds(at, step), :] = (upper << 16) | (pltpu.roll(upper, 64, 1) & 65535)

    @pl.loop(0, count // 16)
    def _(k):
        for u in range(16):
            row = k * 16 + u
            out_ref[pl.ds(pos_ref[1, row], 1), :] = word_ref[pl.ds(row, 1), :]
            sent_ref[pl.ds(pos_ref[0, row], 1), :] = tail_ref[pl.ds(row, 1), :]

    half = cap // 2
    left = lax.broadcasted_iota(jnp.int32, (half, 128), 1) < 64
    for owner in range(sent_ref.shape[0] // cap):
        begin = owner * packed_rows(cap) + cap
        first = sent_ref[owner * cap:owner * cap + half, :]
        second = sent_ref[owner * cap + half:(owner + 1) * cap, :]
        out_ref[begin:begin + half, :] = jnp.where(left, first, pltpu.roll(second, 64, 1))
        out_ref[begin + half:begin + half + 8, :] = jnp.broadcast_to(exponent, (8, 128))


def project(tri, start, x, pos, owners, cap):
    feature, width = start.shape
    return pl.pallas_call(
        functools.partial(project_kernel, cap),
        out_shape=(
            jax.ShapeDtypeStruct((owners * packed_rows(cap), 128), jnp.int32),
            jax.ShapeDtypeStruct((feature, 2 * width), jnp.bfloat16),
            jax.ShapeDtypeStruct((width, width), jnp.float32),
        ),
        in_specs=[vmem(), vmem(), pl.BlockSpec(memory_space=pl.ANY), smem()],
        out_specs=(vmem(), vmem(), vmem()),
        scratch_shapes=[
            pltpu.VMEM(x.shape, jnp.bfloat16),
            pltpu.SemaphoreType.DMA,
            pltpu.VMEM((feature, feature), jnp.bfloat16),
            pltpu.VMEM((feature, feature), jnp.bfloat16),
            pltpu.VMEM((2 * x.shape[0], 128), jnp.float32),
            pltpu.VMEM((x.shape[0], 128), jnp.int32),
            pltpu.VMEM((x.shape[0], 128), jnp.int32),
            pltpu.VMEM((owners * cap, 128), jnp.int32),
        ],
        compiler_params=limits(),
        cost_estimate=pl.CostEstimate(flops=10**10, bytes_accessed=2 * 10**7, transcendentals=0),
        name="project",
    )(tri, start, x, pos)


def factor_kernel(gram_ref, inverse_ref, pivot_ref, aug):
    size = gram_ref.shape[0]
    block = 32
    panel = 8
    aug[:, :size] = gram_ref[...]
    aug[:, size:] = (
        lax.broadcasted_iota(jnp.int32, (size, size), 0) == lax.broadcasted_iota(jnp.int32, (size, size), 1)
    ).astype(jnp.float32)
    row_at = lax.broadcasted_iota(jnp.int32, (block, 128), 0)
    lane_at = lax.broadcasted_iota(jnp.int32, (block, 128), 1)
    least = jnp.full((1, 128), 1e30, jnp.float32)
    for b in range(size // block):
        lo, hi = b * block, (b + 1) * block
        square = aug[lo:hi, lo:hi]
        unit = (row_at[:, :block] == lane_at[:, :block]).astype(jnp.float32)
        work = jnp.concatenate([square, unit, jnp.zeros((block, 128 - 2 * block), jnp.float32)], axis=1)
        for p in range(block // panel):
            cols = [
                jnp.broadcast_to(work[:, p * panel + j:p * panel + j + 1], (block, 128)) for j in range(panel)
            ]
            for j in range(panel):
                k = p * panel + j
                pivot = cols[j][k:k + 1, :]
                least = jnp.minimum(least, pivot)
                root = lax.rsqrt(pivot)
                column = jnp.where(row_at > k, cols[j] * root, 0.0)
                for jj in range(j + 1, panel):
                    kk = p * panel + jj
                    cols[jj] = cols[jj] - column * column[kk:kk + 1, :]
                row = work[k:k + 1, :] * root
                work = jnp.where(row_at == k, row, work - column * row)
        inverse = work[:, block:2 * block]
        rows = lax.dot_general(inverse, aug[lo:hi, :], (((1,), (0,)), ((), ())), precision=lax.Precision.HIGHEST,
                               preferred_element_type=jnp.float32)
        aug[lo:hi, :] = rows
        if hi < size:
            below = rows[:, hi:size].T
            aug[hi:, :] -= lax.dot_general(below, rows, (((1,), (0,)), ((), ())), precision=lax.Precision.HIGHEST,
                                           preferred_element_type=jnp.float32)
    whole = aug[:, size:].T
    top, bottom = halves(whole)
    inverse_ref[:, :size] = top
    inverse_ref[:, size:] = bottom
    pivot_ref[...] = least


def factor(gram):
    size = gram.shape[0]
    return pl.pallas_call(
        factor_kernel,
        out_shape=(
            jax.ShapeDtypeStruct((size, 2 * size), jnp.bfloat16),
            jax.ShapeDtypeStruct((1, 128), jnp.float32),
        ),
        in_specs=[vmem()],
        out_specs=(vmem(), vmem()),
        scratch_shapes=[pltpu.VMEM((size, 2 * size), jnp.float32)],
        compiler_params=limits(),
        cost_estimate=pl.CostEstimate(flops=10**9, bytes_accessed=10**7, transcendentals=0),
        name="factor",
    )(gram)


def offset_kernel(cap, c_ref, basis_ref, id_ref, out_ref, z_ref):
    project_rows(c_ref, basis_ref, z_ref)
    count = c_ref.shape[0]

    @pl.loop(0, id_ref.shape[0] // cap)
    def _(sender):
        @pl.loop(0, cap // 16)
        def _(k):
            for u in range(16):
                rank = k * 16 + u
                row = jnp.maximum(id_ref[sender * cap + rank], 0)
                slot = sender * (2 * cap) + rank
                out_ref[pl.ds(slot, 1), :] = z_ref[pl.ds(row, 1), :]
                out_ref[pl.ds(slot + cap, 1), :] = z_ref[pl.ds(row + count, 1), :]


def offsets_at(centroids, basis, ids, cap):
    return pl.pallas_call(
        functools.partial(offset_kernel, cap),
        out_shape=jax.ShapeDtypeStruct((2 * ids.shape[0], 128), jnp.float32),
        in_specs=[vmem(), vmem(), smem()],
        out_specs=vmem(),
        scratch_shapes=[pltpu.VMEM((2 * centroids.shape[0], 128), jnp.float32)],
        compiler_params=limits(),
        cost_estimate=pl.CostEstimate(flops=10**10, bytes_accessed=10**7, transcendentals=0),
        name="offsets",
    )(centroids, basis, ids)


def finish_kernel(senders, z_ref, off_ref, count_ref, inverse_ref, out_ref):
    width = out_ref.shape[1]
    cap = out_ref.shape[0] // senders
    rank = lax.broadcasted_iota(jnp.int32, (cap, width), 0)
    half = cap // 2
    left = lax.broadcasted_iota(jnp.int32, (half, 128), 1) < 64
    gaps = []
    for s in range(senders):
        begin = s * packed_rows(cap)
        word = z_ref[begin:begin + cap, :]
        tail = z_ref[begin + cap:begin + cap + half, :]
        unit = step_of(z_ref[begin + cap + half:begin + cap + half + 1, :])
        upper = tail >> 16
        under = (tail << 16) >> 16
        first = jnp.where(left, upper, pltpu.roll(under, 64, 1))
        second = jnp.where(left, pltpu.roll(upper, 64, 1), under)
        high = (jnp.concatenate([first, second], axis=0) << 8) | (word & 255)
        begin = 2 * s * cap
        low = (word >> 8).astype(jnp.float32) * unit - off_ref[begin:begin + cap, :]
        high = high.astype(jnp.float32) * unit - off_ref[begin + cap:begin + 2 * cap, :]
        gaps.append(jnp.concatenate([low, high], axis=1))
    hi, lo = halves(jnp.concatenate(gaps, axis=0))
    both = dot(hi, inverse_ref[...])
    code = (both[:, :width] + both[:, width:]) + dot(lo, inverse_ref[:, :width])
    for s in range(senders):
        filled = rank < count_ref[pl.program_id(0) * senders + s]
        at = slice(s * cap, (s + 1) * cap)
        out_ref[at, :] = jnp.where(filled, code[at, :], 0.0).astype(jnp.bfloat16)


def finish(z, off, filled, inverse):
    owners = filled.shape[0]
    slots = off.shape[0] // 2
    width = inverse.shape[0]
    senders = 8
    step = senders * (slots // owners)
    return pl.pallas_call(
        functools.partial(finish_kernel, senders),
        out_shape=jax.ShapeDtypeStruct((slots, width), jnp.bfloat16),
        grid=(slots // step,),
        in_specs=[
            pl.BlockSpec((z.shape[0] // owners * senders, 128), lambda s: (s, 0)),
            pl.BlockSpec((2 * step, 128), lambda s: (s, 0)),
            smem(),
            pl.BlockSpec((width, 2 * width), lambda s: (0, 0)),
        ],
        out_specs=pl.BlockSpec((step, width), lambda s: (s, 0)),
        compiler_params=limits(),
        cost_estimate=pl.CostEstimate(flops=2 * 10**9, bytes_accessed=13 * 10**6, transcendentals=0),
        name="finish",
    )(z, off, filled, inverse)


exact_mode = lax.Precision.HIGHEST
PIVOT_LEAST = 1.0 / 64.0


def orthonormal(product):
    gram_matrix = jnp.dot(product.T, product, precision=exact_mode, preferred_element_type=jnp.float32)
    lower = jnp.linalg.cholesky(gram_matrix)
    return jax.scipy.linalg.solve_triangular(lower, product.T, lower=True).T


def careful(tri, start, x, centroids, pos, ids):
    owners = lax.axis_size("dev")
    slots = ids.shape[0]
    grid = [[None] * 8 for _ in range(8)]
    for i in range(8):
        for j in range(i + 1):
            at = STARTS[(i, j)]
            grid[i][j] = tri[at:at + 128]
            grid[j][i] = tri[at:at + 128].T
    moment = jnp.block(grid)
    basis = start
    for sweep in range(2):
        product = jnp.dot(moment, basis, precision=exact_mode, preferred_element_type=jnp.float32)
        basis = orthonormal(product)
    width = start.shape[1]
    projected = jnp.dot(x, basis, precision=exact_mode, preferred_element_type=jnp.float32)
    sent = jnp.zeros((slots, width), jnp.float32).at[pos[0]].set(projected)
    sent = sent.reshape(owners, slots // owners, width)
    values = lax.all_to_all(sent, "dev", split_axis=0, concat_axis=0, tiled=True).reshape(slots, width)
    offsets = jnp.dot(centroids, basis, precision=exact_mode, preferred_element_type=jnp.float32)
    code = values - jnp.take(offsets, jnp.maximum(ids, 0), axis=0)
    return jnp.where(ids[:, None] >= 0, code, 0.0).astype(jnp.bfloat16)


def shards(corpus_rows, list_ids, source_ids, list_slot, centroids, start_basis):
    owners = lax.axis_size("dev")
    lists_dev = centroids.shape[0]
    slots = owners * CAP
    tri, pos, arrived, counts = front(corpus_rows, list_ids, source_ids, list_slot, owners, lists_dev, CAP)
    sent, basis, gram = project(tri, start_basis, corpus_rows, pos, owners, CAP)
    values = lax.all_to_all(
        sent.reshape(owners, packed_rows(CAP), 128), "dev", split_axis=0, concat_axis=0, tiled=True
    ).reshape(owners * packed_rows(CAP), 128)
    ids = arrived[:, :2].reshape(owners, 256)[:, :CAP]
    filled = jnp.sum((ids >= 0).astype(jnp.int32), axis=1)
    ids = ids.reshape(slots)
    row_sources = arrived[:, 2:].reshape(owners, 256)[:, :CAP].reshape(slots)
    inverse, pivots = factor(gram)
    off = offsets_at(centroids, basis, ids, CAP)
    row_codes = lax.cond(
        jnp.min(pivots) >= PIVOT_LEAST,
        lambda codes: codes,
        lambda codes: careful(tri, start_basis, corpus_rows, centroids, pos, ids),
        finish(values, off, filled, inverse),
    )
    return row_codes, row_sources, counts.reshape(lists_dev)


def solution(mesh):
    placed = (
        P(("group", "dev"), None),
        P(("group", "dev")),
        P(("group", "dev")),
        P(),
        P("dev", None),
        P(),
    )
    return jax.shard_map(
        shards,
        mesh=mesh,
        in_specs=placed,
        out_specs=(P(("group", "dev"), None), P(("group", "dev")), P("dev")),
        check_vma=False,
    )
```
